32 devices in a mesh: row: 8 (over y, x, core), col: 4 (over z).
Axes of the slice: x: 2, y: 2, z: 4, core: 2. Of those that a mesh axis runs over, the one named last changes fastest.
Arguments:
- tile_blocks: bfloat16 [768, 128, 128], P(('row', 'col')), may hold values from -0.21875 to 0.21875
- tile_rows: int32 [768], P(('row', 'col')), may hold values from 0 to 255, as said below
- tile_cols: int32 [768], P(('row', 'col')), may hold values from 0 to 255, as said below
- trial_vectors: bfloat16 [4, 32768], P(None, ('col', 'row')), may hold values from -6 to 6
- basis_old: float32 [44, 32768], P(None, ('col', 'row'))
- image_old: float32 [44, 32768], P(None, ('col', 'row'))
Outputs:
- projected: float32 [48, 48], replicated
- basis_new: float32 [48, 32768], P(None, ('col', 'row'))
- image_new: float32 [48, 32768], P(None, ('col', 'row'))
The draws below stay inside these ranges and needn't reach their ends.
Inputs may be any that keep to these rules, and one draw needn't show every extreme that they name: `tile_rows`: the 24 tiles of each device with index r on row have block rows b for which (b // 8) % 8 equals r. `tile_cols`: the 24 tiles of each device with index c on col have block columns from c * 64 to (c + 1) * 64 - 1.
All inputs are finite; a program needn't handle non-finite values.
Results may differ from the reference program's by a relative error of at most 0.0003.
Values may be sent and summed in bfloat16 or wider, within the bound.
No kernel may reach another device: no remote copies, remote signals or barrier semaphores. Data moves between devices by JAX's collectives and lax.ppermute only.
A program may use at most 64 MiB of HBM per device.

```python
import math
import jax
import jax.numpy as jnp
from jax import lax

TILE = 128
NVEC = 4
NOLD = 44
BLK = 8
KT = 24
NB = 256
ORDER = 32768
RB = 32
CB = 64
TILES = 768


def basis_pair(key):
    key_scale = jax.random.fold_in(key, 31)
    key_base = jax.random.fold_in(key, 32)
    key_gain = jax.random.fold_in(key, 33)
    key_noise = jax.random.fold_in(key, 34)
    position = jnp.arange(ORDER, dtype=jnp.float32) / float(ORDER)
    spread = jax.random.uniform(key_scale, (ORDER,), jnp.float32, 0.0, math.log(10.0))
    column_scale = (1.0 + 2.0 * position) * jnp.exp(spread)
    base = jax.random.normal(key_base, (NOLD, ORDER), jnp.float32)
    noise = jax.random.normal(key_noise, (NOLD, ORDER), jnp.float32)
    gains = jnp.exp(jax.random.uniform(key_gain, (NOLD, 1), jnp.float32, -1.0, 1.0))
    basis = base * column_scale[None, :]
    image = gains * basis + 0.5 * noise * column_scale[None, :]
    return (basis, image)


def draw_basis_old(key, part):
    return basis_pair(key)[0]


def draw_image_old(key, part):
    return basis_pair(key)[1]


def draw_tile_rows(key, part):
    index = jnp.arange(TILES, dtype=jnp.int32)
    device = index // KT
    col_count = RB // BLK
    row_count = CB // BLK
    row_index = device // col_count
    offset = jax.random.randint(jax.random.fold_in(key, 11), (TILES,), 0, RB, dtype=jnp.int32)
    piece_slot = offset // BLK
    inner = offset % BLK
    return ((piece_slot * row_count + row_index) * BLK + inner).astype(jnp.int32)


def draw_tile_cols(key, part):
    index = jnp.arange(TILES, dtype=jnp.int32)
    device = index // KT
    col_count = RB // BLK
    col_index = device % col_count
    offset = jax.random.randint(jax.random.fold_in(key, 12), (TILES,), 0, CB, dtype=jnp.int32)
    return (col_index * CB + offset).astype(jnp.int32)


def shard_levels(stream_key, dims, pieces, smallest, largest):
    level, own = 1.0, jax.random.fold_in(stream_key, 6)
    for dim, blocks in pieces:
        heights = jnp.exp(jax.random.uniform(jax.random.fold_in(own, dim), (blocks,), jnp.float32, smallest / len(pieces), largest / len(pieces)))
        level = level * jnp.repeat(heights, dims[dim] // blocks).reshape([-1 if axis == dim else 1 for axis in range(len(dims))])
    return level


def gaussian(own_key, dims, deviation, most, cuts=(), held_as=jnp.bfloat16):
    array = deviation * jax.random.normal(own_key, dims, jnp.float32)
    if cuts:
        array = array * shard_levels(own_key, dims, cuts, -0.22, 0.18)
    return jnp.clip(array, -most, most).astype(held_as)


def setup_inputs(seed: int = 0) -> dict:
    streams_of = jax.random.split(jax.random.key(seed), 7)
    return {
        "tile_blocks": gaussian(streams_of[0], (TILES, TILE, TILE), (2 * TILE * KT // BLK) ** -0.5, 0.21875, ((0, 32),)),
        "tile_rows": draw_tile_rows(jax.random.fold_in(streams_of[6], 71), 0),
        "tile_cols": draw_tile_cols(jax.random.fold_in(streams_of[6], 71), 0),
        "trial_vectors": gaussian(streams_of[3], (NVEC, ORDER), 1.0, 6.0, ((1, 32),)),
        "basis_old": draw_basis_old(jax.random.fold_in(streams_of[6], 71), 0),
        "image_old": draw_image_old(jax.random.fold_in(streams_of[6], 71), 0),
    }


def reference(tile_blocks, tile_rows, tile_cols, trial_vectors, basis_old, image_old):
    highest = lax.Precision.HIGHEST
    vec_blocks = trial_vectors.astype(jnp.float32).reshape(NVEC, NB, TILE)

    def per_device(items):
        blocks, rows_here, cols_here = items
        wide_blocks = blocks.astype(jnp.float32)
        forward = jnp.einsum('ktb,tab->tka', vec_blocks[:, cols_here], wide_blocks, precision=highest)
        backward = jnp.einsum('kta,tab->tkb', vec_blocks[:, rows_here], wide_blocks, precision=highest)
        return (forward, backward)
    device_count = TILES // KT
    forward, backward = lax.map(per_device, (tile_blocks.reshape(device_count, KT, TILE, TILE), tile_rows.reshape(device_count, KT), tile_cols.reshape(device_count, KT)))
    sums = jax.ops.segment_sum(forward.reshape(TILES, NVEC, TILE), tile_rows, NB)
    sums = sums + jax.ops.segment_sum(backward.reshape(TILES, NVEC, TILE), tile_cols, NB)
    image = sums.transpose(1, 0, 2).reshape(NVEC, ORDER)
    basis_all = jnp.concatenate([basis_old, trial_vectors.astype(jnp.float32)], axis=0)
    images_all = jnp.concatenate([image_old, image], axis=0)
    correlation = jnp.dot(basis_all, basis_all.T, precision=highest) / float(ORDER)
    coupling = jnp.dot(basis_all, images_all.T, precision=highest) / float(ORDER)
    factor = jnp.linalg.cholesky(correlation)

    def solve_lower(matrix):
        return lax.linalg.triangular_solve(factor, matrix, left_side=True, lower=True)
    half_done = solve_lower(coupling)
    projected = solve_lower(half_done.T).T
    return (projected, solve_lower(basis_all), solve_lower(images_all))
```

```python
import functools

import jax
import jax.numpy as jnp
from jax import lax
from jax.experimental import pallas as pl
from jax.experimental.pallas import tpu as pltpu
from jax.sharding import PartitionSpec as P

HIGHEST = lax.Precision.HIGHEST
LANES = 128
VMEM_LIMIT = 32 * 1024 * 1024


def contract_last(left, right):
    return lax.dot_general(
        left,
        right,
        (((1,), (1,)), ((), ())),
        precision=HIGHEST,
        preferred_element_type=jnp.float32,
    )


def multiply(left, right):
    return jnp.dot(left, right, precision=HIGHEST, preferred_element_type=jnp.float32)


def side_by_side(blocks_ref):
    return jnp.concatenate([blocks_ref[b] for b in range(blocks_ref.shape[0])], axis=1)


def gram_kernel(scale, trial_ref, basis_ref, image_ref, wide_ref, gram_ref):
    trial = trial_ref[...].astype(jnp.float32)
    for b in range(wide_ref.shape[0]):
        wide_ref[b] = trial[:, b * LANES : (b + 1) * LANES]
    basis_all = jnp.concatenate([basis_ref[...], trial], axis=0)
    correlation = contract_last(basis_all, basis_all)
    coupling = contract_last(basis_all, image_ref[...])
    count = correlation.shape[0]
    unused = jnp.zeros((count, LANES - count - coupling.shape[1]), jnp.float32)
    gram = jnp.concatenate([correlation, coupling, unused], axis=1) * scale
    vecs = gram_ref.shape[1]
    for i in range(gram_ref.shape[0]):
        gram_ref[i] = gram[i * vecs : (i + 1) * vecs]


def tiles_kernel(index_ref, tiles_ref, col_vecs_ref, row_vecs_ref, row_sums_ref, col_sums_ref):
    row_sums_ref[...] = jnp.zeros_like(row_sums_ref)
    col_sums_ref[...] = jnp.zeros_like(col_sums_ref)
    for t in range(tiles_ref.shape[0]):
        tile = tiles_ref[t]
        by_cols = col_vecs_ref[index_ref[0, t]].astype(jnp.bfloat16)
        by_rows = row_vecs_ref[index_ref[1, t]].astype(jnp.bfloat16)
        forward = lax.dot_general(
            by_cols, tile, (((1,), (1,)), ((), ())), preferred_element_type=jnp.float32
        )
        backward = jnp.dot(by_rows, tile, preferred_element_type=jnp.float32)
        to_row, to_col = index_ref[2, t], index_ref[3, t]
        row_sums_ref[to_row] = row_sums_ref[to_row] + forward
        col_sums_ref[to_col] = col_sums_ref[to_col] + backward


def factor_kernel(count, gram_ref, inverse_ref, start_ref):
    gram = jnp.concatenate([gram_ref[i] for i in range(gram_ref.shape[0])], axis=0)
    row_id = lax.broadcasted_iota(jnp.int32, (count, LANES), 0)
    lane_id = lax.broadcasted_iota(jnp.int32, (count, LANES), 1)
    identity = jnp.where(lane_id == row_id + count, 1.0, 0.0)
    work = jnp.where(lane_id < count, gram, identity)
    diagonal = jnp.ones((count, 1), jnp.float32)
    for j in range(count):
        pivot_row = work[j : j + 1, :]
        pivot = work[j : j + 1, j : j + 1]
        column = work[:, j : j + 1]
        below = row_id[:, :1] > j
        ratio = jnp.where(below, column / pivot, 0.0)
        diagonal = jnp.where(row_id[:, :1] == j, pivot, diagonal)
        work = work - ratio * pivot_row
    inverse = work[:, count : 2 * count] * lax.rsqrt(diagonal)
    old = count - gram_ref.shape[1]
    coupling = gram[:, count : count + old]
    inverse_ref[...] = inverse
    start_ref[...] = contract_last(multiply(inverse, coupling), inverse[:, :old])


def image_kernel(
    scale, inverse_ref, wide_ref, basis_ref, image_ref, rows_ref, cols_ref, basis_new_ref, image_new_ref, part_ref
):
    inverse = inverse_ref[...]
    basis_new = multiply(inverse, jnp.concatenate([basis_ref[...], side_by_side(wide_ref)], axis=0))
    basis_new_ref[...] = basis_new
    summed = [rows_ref[b] + cols_ref[b] for b in range(rows_ref.shape[0])]
    image = jnp.concatenate(summed, axis=1)
    vecs, count = image.shape[0], inverse.shape[0]
    part = contract_last(image, basis_new) * scale
    part = jnp.concatenate([part, jnp.zeros((vecs, LANES - count), jnp.float32)], axis=1)
    part_ref[...] = jnp.broadcast_to(part[None], part_ref.shape)
    image_new_ref[...] = multiply(inverse, jnp.concatenate([image_ref[...], image], axis=0))


def project_kernel(inverse_ref, start_ref, parts_ref, projected_ref):
    total = jnp.sum(parts_ref[...], axis=0)
    vecs = total.shape[0]
    count = inverse_ref.shape[0]
    last = inverse_ref[...][:, count - vecs :]
    new = lax.dot_general(
        total[:, :count],
        last,
        (((0,), (1,)), ((), ())),
        precision=HIGHEST,
        preferred_element_type=jnp.float32,
    )
    projected_ref[...] = start_ref[...] + new


def call(kernel, outs, *args, smem=(), flops=0):
    in_specs = [
        pl.BlockSpec(memory_space=pltpu.SMEM if i in smem else pltpu.VMEM) for i in range(len(args))
    ]
    many = isinstance(outs, (list, tuple))
    return pl.pallas_call(
        kernel,
        out_shape=[jax.ShapeDtypeStruct(o, jnp.float32) for o in outs],
        in_specs=in_specs,
        out_specs=[pl.BlockSpec(memory_space=pltpu.VMEM)] * len(outs),
        compiler_params=pltpu.CompilerParams(vmem_limit_bytes=VMEM_LIMIT),
        cost_estimate=pl.CostEstimate(flops=flops, bytes_accessed=0, transcendentals=0),
    )(*args)


def bits_of(size):
    return [1 << j for j in range(size.bit_length() - 1)]


def swap(array, axis, mask):
    size = lax.axis_size(axis)
    return lax.ppermute(array, axis, [(i, i ^ mask) for i in range(size)])


def place(apart, bits):
    return sum(((apart // m) % 2) * (1 << j) for j, m in enumerate(bits))


def local(tile_blocks, tile_rows, tile_cols, trial_vectors, basis_old, image_old):
    tile_size = tile_blocks.shape[1]
    vecs, width = trial_vectors.shape
    old = basis_old.shape[0]
    count = old + vecs
    blocks = width // tile_size
    n_row, n_col = lax.axis_size("row"), lax.axis_size("col")
    row, col = lax.axis_index("row"), lax.axis_index("col")
    scale = 1.0 / float(width * n_row * n_col)
    row_bits, col_bits = bits_of(n_row), bits_of(n_col)

    gather_row = row_bits[1:] + row_bits[:1]
    gather_col = col_bits
    scatter_row = row_bits
    scatter_col = col_bits
    row_piece = tile_rows // blocks // n_row
    row_inner = tile_rows % blocks
    local_col = tile_cols - col * (blocks * n_row)
    col_piece, col_inner = local_col // blocks, local_col % blocks
    row_apart = row_piece ^ col
    col_apart = col_piece ^ row
    index = jnp.stack(
        [
            place(col_apart, gather_row) * blocks + col_inner,
            place(row_apart, gather_col) * blocks + row_inner,
            place(row_apart, scatter_col[::-1]) * blocks + row_inner,
            place(col_apart, scatter_row[::-1]) * blocks + col_inner,
        ]
    )

    wide, gram = call(
        functools.partial(gram_kernel, scale),
        [(blocks, vecs, tile_size), (count // vecs, vecs, LANES)],
        trial_vectors,
        basis_old,
        image_old,
    )
    col_vecs = wide
    for m in gather_row:
        col_vecs = jnp.concatenate([col_vecs, swap(col_vecs, "row", m)], axis=0)
    row_vecs = wide
    for m in gather_col:
        size = row_vecs.shape[0]
        got = swap(jnp.concatenate([row_vecs, gram], axis=0), "col", m)
        row_vecs = jnp.concatenate([row_vecs, got[:size]], axis=0)
        gram = gram + got[size:]

    row_sums, col_sums = call(
        tiles_kernel,
        [(blocks * n_col, vecs, tile_size), (blocks * n_row, vecs, tile_size)],
        index,
        tile_blocks,
        col_vecs,
        row_vecs,
        smem=(0,),
    )
    for m in scatter_row:
        half = col_sums.shape[0] // 2
        got = swap(jnp.concatenate([col_sums[half:], gram], axis=0), "row", m)
        col_sums = col_sums[:half] + got[:half]
        gram = gram + got[half:]
    for m in scatter_col:
        half = row_sums.shape[0] // 2
        row_sums = row_sums[:half] + swap(row_sums[half:], "col", m)

    inverse, start = call(
        functools.partial(factor_kernel, count), [(count, count), (count, count)], gram
    )
    basis_new, image_new, part = call(
        functools.partial(image_kernel, scale),
        [(count, width), (count, width), (n_row * n_col, vecs, LANES)],
        inverse,
        wide,
        basis_old,
        image_old,
        row_sums,
        col_sums,
    )
    parts = lax.all_to_all(part, ("row", "col"), split_axis=0, concat_axis=0, tiled=True)
    (projected,) = call(project_kernel, [(count, count)], inverse, start, parts)
    return projected, basis_new, image_new


def solution(mesh):
    in_specs = (
        P(("row", "col"), None, None),
        P(("row", "col")),
        P(("row", "col")),
        P(None, ("col", "row")),
        P(None, ("col", "row")),
        P(None, ("col", "row")),
    )
    out_specs = (P(), P(None, ("col", "row")), P(None, ("col", "row")))
    return jax.shard_map(local, mesh=mesh, in_specs=in_specs, out_specs=out_specs, check_vma=False)
```

```python
import functools

import jax
import jax.numpy as jnp
from jax import lax
from jax.experimental import pallas as pl
from jax.experimental.pallas import tpu as pltpu
from jax.sharding import PartitionSpec as P

HIGHEST = lax.Precision.HIGHEST
LANES = 128
SUBLANES = 8
PANEL = 16
VMEM_LIMIT = 32 * 1024 * 1024


def contract_last(left, right):
    return lax.dot_general(
        left,
        right,
        (((1,), (1,)), ((), ())),
        precision=HIGHEST,
        preferred_element_type=jnp.float32,
    )


def multiply(left, right):
    return jnp.dot(left, right, precision=HIGHEST, preferred_element_type=jnp.float32)


def side_by_side(blocks_ref):
    return jnp.concatenate([blocks_ref[b] for b in range(blocks_ref.shape[0])], axis=1)


def load_kernel(
    trial_hbm, basis_hbm, image_hbm, rows_hbm, cols_hbm,
    wide_ref, basis_ref, image_ref, rows_ref, cols_ref, trial_vmem, basis_vmem, sems,
):
    copies = [
        pltpu.make_async_copy(source, target, sems.at[i])
        for i, (source, target) in enumerate(
            [
                (trial_hbm, trial_vmem),
                (basis_hbm, basis_vmem),
                (image_hbm, image_ref),
                (rows_hbm, rows_ref),
                (cols_hbm, cols_ref),
            ]
        )
    ]
    for copy in copies:
        copy.start()
    copies[0].wait()
    trial = trial_vmem[...].astype(jnp.float32)
    for b in range(wide_ref.shape[0]):
        wide_ref[b] = trial[:, b * LANES : (b + 1) * LANES]
    copies[1].wait()
    basis_ref[...] = jnp.concatenate([basis_vmem[...], trial], axis=0)
    for copy in copies[2:]:
        copy.wait()


def gram_kernel(scale, wide_ref, basis_ref, image_ref, sent_ref):
    blocks, vecs = wide_ref.shape[:2]
    basis_all = basis_ref[...]
    correlation = contract_last(basis_all, basis_all)
    coupling = contract_last(basis_all, image_ref[...])
    count = correlation.shape[0]
    unused = jnp.zeros((count, LANES - count - coupling.shape[1]), jnp.float32)
    gram = jnp.concatenate([correlation, coupling, unused], axis=1) * scale
    sent_ref[:blocks] = wide_ref[...]
    for i in range(sent_ref.shape[0] - blocks):
        sent_ref[blocks + i] = gram[i * vecs : (i + 1) * vecs]


def split(index, size):
    return index >> (size.bit_length() - 1), index & (size - 1)


def place(apart, bits):
    if bits == bits_of(1 << len(bits)):
        return apart
    return sum(((apart >> (m.bit_length() - 1)) & 1) << j for j, m in enumerate(bits))


def tiles_kernel(
    contract, by_rows, by_cols, n_row, blocks, position_ref, rows_ref, cols_ref, tiles_ref, vecs_ref, sums_ref
):
    sums_ref[...] = jnp.zeros_like(sums_ref)
    row, col = position_ref[0], position_ref[1]
    for t in range(tiles_ref.shape[0]):
        row_piece, row_inner = split(rows_ref[t], blocks)
        col_piece, col_inner = split(cols_ref[t] - col * (blocks * n_row), blocks)
        at_row = place(split(row_piece, n_row)[0] ^ col, by_rows) * blocks + row_inner
        at_col = place(col_piece ^ row, by_cols) * blocks + col_inner
        source, target = (at_col, at_row) if contract else (at_row, at_col)
        product = lax.dot_general(
            vecs_ref[source].astype(jnp.bfloat16),
            tiles_ref[t],
            (((1,), (contract,)), ((), ())),
            preferred_element_type=jnp.float32,
        )
        sums_ref[target] = sums_ref[target] + product


def factor_kernel(count, gram_ref, inverse_ref):
    gram = jnp.concatenate([gram_ref[i] for i in range(gram_ref.shape[0])], axis=0)
    row_id = lax.broadcasted_iota(jnp.int32, (count, LANES), 0)
    lane_id = lax.broadcasted_iota(jnp.int32, (count, LANES), 1)
    identity = jnp.where(lane_id == row_id + count, 1.0, 0.0)
    work = jnp.where(lane_id < count, gram, identity)
    tiles = count // SUBLANES
    work = [work[SUBLANES * g : SUBLANES * (g + 1)] for g in range(tiles)]
    sublane = lax.broadcasted_iota(jnp.int32, (SUBLANES, LANES), 0)
    diagonal = [jnp.ones((SUBLANES, LANES), jnp.float32)] * tiles

    def spread(tile, i):
        return jnp.broadcast_to(tile[i : i + 1, :], (SUBLANES, LANES))

    for start in range(0, count, PANEL):
        stop = min(start + PANEL, count)
        first = start // SUBLANES
        columns = {
            j: {
                g: jnp.broadcast_to(work[g][:, j : j + 1], (SUBLANES, LANES))
                for g in range(first, tiles)
            }
            for j in range(start, stop)
        }
        for j in range(start, stop):
            i, own = j % SUBLANES, j // SUBLANES
            pivot = spread(columns[j][own], i)
            diagonal[own] = jnp.where(sublane == i, pivot, diagonal[own])
            reciprocal = 1.0 / pivot
            row = spread(work[own], i)
            entries = {k: spread(columns[k][own], i) for k in range(j + 1, stop)}
            for g in range(own, tiles):
                ratio = columns[j][g] * reciprocal
                if g == own:
                    ratio = jnp.where(sublane > i, ratio, 0.0)
                work[g] = work[g] - ratio * row
                for k in range(j + 1, stop):
                    columns[k][g] = columns[k][g] - ratio * entries[k]
    for g in range(tiles):
        scaled = work[g] * lax.rsqrt(diagonal[g])
        inverse_ref[SUBLANES * g : SUBLANES * (g + 1), :] = scaled[:, count : 2 * count]


def basis_kernel(inverse_ref, gram_ref, basis_ref, image_ref, basis_new_ref, image_start_ref, start_ref):
    inverse = inverse_ref[...]
    count, old = inverse.shape[0], image_ref.shape[0]
    basis_new_ref[...] = multiply(inverse, basis_ref[...])
    image_start_ref[...] = multiply(inverse[:, :old], image_ref[...])
    gram = jnp.concatenate([gram_ref[i] for i in range(gram_ref.shape[0])], axis=0)
    coupling = gram[:, count : count + old]
    start_ref[...] = contract_last(multiply(inverse, coupling), inverse[:, :old])


def image_kernel(scale, basis_new_ref, rows_ref, cols_ref, image_ref, part_ref):
    summed = [rows_ref[b] + cols_ref[b] for b in range(rows_ref.shape[0])]
    image = jnp.concatenate(summed, axis=1)
    image_ref[...] = image
    vecs, count = image.shape[0], basis_new_ref.shape[0]
    part = contract_last(image, basis_new_ref[...]) * scale
    part = jnp.concatenate([part, jnp.zeros((vecs, LANES - count), jnp.float32)], axis=1)
    part_ref[...] = jnp.broadcast_to(part[None], part_ref.shape)


def finish_kernel(
    inverse_ref, basis_new_ref, image_start_ref, image_ref, start_ref, parts_ref,
    projected_hbm, basis_new_hbm, image_new_hbm, projected_vmem, image_new_vmem, sems,
):
    basis_copy = pltpu.make_async_copy(basis_new_ref, basis_new_hbm, sems.at[0])
    basis_copy.start()
    vecs = image_ref.shape[0]
    count = inverse_ref.shape[0]
    last = inverse_ref[...][:, count - vecs :]
    image_new_vmem[...] = image_start_ref[...] + multiply(last, image_ref[...])
    image_copy = pltpu.make_async_copy(image_new_vmem, image_new_hbm, sems.at[1])
    image_copy.start()
    total = jnp.sum(parts_ref[...], axis=0)
    new = lax.dot_general(
        total[:, :count],
        last,
        (((0,), (1,)), ((), ())),
        precision=HIGHEST,
        preferred_element_type=jnp.float32,
    )
    projected_vmem[...] = start_ref[...] + new
    projected_copy = pltpu.make_async_copy(projected_vmem, projected_hbm, sems.at[2])
    projected_copy.start()
    basis_copy.wait()
    image_copy.wait()
    projected_copy.wait()


def call(kernel, outs, *args, smem=0, from_hbm=False, to_hbm=False, scratch=(), flops=0):
    operand = pl.BlockSpec(memory_space=pltpu.HBM if from_hbm else pltpu.VMEM)
    result = pl.BlockSpec(memory_space=pltpu.HBM if to_hbm else pltpu.VMEM)
    scalars = pl.BlockSpec(memory_space=pltpu.SMEM)
    if from_hbm:
        args = [pltpu.with_memory_space_constraint(arg, pltpu.HBM) for arg in args]
    outs = [o if hasattr(o, "dtype") else jax.ShapeDtypeStruct(o, jnp.float32) for o in outs]
    return pl.pallas_call(
        kernel,
        out_shape=outs,
        in_specs=[scalars] * smem + [operand] * (len(args) - smem),
        out_specs=[result] * len(outs),
        scratch_shapes=scratch,
        compiler_params=pltpu.CompilerParams(vmem_limit_bytes=VMEM_LIMIT),
        cost_estimate=pl.CostEstimate(flops=flops, bytes_accessed=0, transcendentals=0),
    )(*args)


def bits_of(size):
    return [1 << j for j in range(size.bit_length() - 1)]


def swap(array, axis, mask):
    size = lax.axis_size(axis)
    return lax.ppermute(array, axis, [(i, i ^ mask) for i in range(size)])


def local(tile_blocks, tile_rows, tile_cols, trial_vectors, basis_old, image_old):
    tile_size = tile_blocks.shape[1]
    vecs, width = trial_vectors.shape
    old = basis_old.shape[0]
    count = old + vecs
    blocks = width // tile_size
    n_row, n_col = lax.axis_size("row"), lax.axis_size("col")
    row, col = lax.axis_index("row"), lax.axis_index("col")
    scale = 1.0 / float(width * n_row * n_col)
    row_bits, col_bits = bits_of(n_row), bits_of(n_col)
    gather_row = row_bits[1:] + row_bits[:1]
    gather_col = col_bits
    scatter_row = row_bits
    scatter_col = col_bits
    grams = count // vecs
    position = jnp.stack([row, col])

    places = jax.ShapeDtypeStruct(tile_rows.shape, tile_rows.dtype)
    wide, basis_all, image_kept, rows_kept, cols_kept = call(
        load_kernel,
        [(blocks, vecs, tile_size), (count, width), (old, width), places, places],
        trial_vectors,
        basis_old,
        image_old,
        tile_rows,
        tile_cols,
        from_hbm=True,
        scratch=[
            pltpu.VMEM((vecs, width), trial_vectors.dtype),
            pltpu.VMEM((old, width), jnp.float32),
            pltpu.SemaphoreType.DMA((5,)),
        ],
    )
    col_vecs = wide
    for m in gather_row:
        col_vecs = jnp.concatenate([col_vecs, swap(col_vecs, "row", m)], axis=0)
    (sent,) = call(
        functools.partial(gram_kernel, scale),
        [(blocks + grams, vecs, LANES)],
        wide,
        basis_all,
        image_kept,
    )
    for m in gather_col:
        size = sent.shape[0] - grams
        got = swap(sent, "col", m)
        gram = sent[size:] + got[size:]
        sent = jnp.concatenate([sent[:size], got[:size], gram], axis=0)

    (col_sums,) = call(
        functools.partial(tiles_kernel, 0, gather_col, scatter_row[::-1], n_row, blocks),
        [(blocks * n_row, vecs, tile_size)],
        position,
        rows_kept,
        cols_kept,
        tile_blocks,
        sent,
        smem=3,
    )
    (row_sums,) = call(
        functools.partial(tiles_kernel, 1, scatter_col[::-1], gather_row, n_row, blocks),
        [(blocks * n_col, vecs, tile_size)],
        position,
        rows_kept,
        cols_kept,
        tile_blocks,
        col_vecs,
        smem=3,
    )
    for m in scatter_row:
        half = col_sums.shape[0] // 2
        got = swap(jnp.concatenate([col_sums[half:], gram], axis=0), "row", m)
        col_sums = col_sums[:half] + got[:half]
        gram = gram + got[half:]
    for m in scatter_col:
        half = row_sums.shape[0] // 2
        row_sums = row_sums[:half] + swap(row_sums[half:], "col", m)

    (inverse,) = call(functools.partial(factor_kernel, count), [(count, count)], gram)
    basis_new, image_start, start = call(
        basis_kernel,
        [(count, width), (count, width), (count, count)],
        inverse,
        gram,
        basis_all,
        image_kept,
    )
    image, part = call(
        functools.partial(image_kernel, scale),
        [(vecs, width), (n_row * n_col, vecs, LANES)],
        basis_new,
        row_sums,
        col_sums,
    )
    parts = lax.all_to_all(part, ("row", "col"), split_axis=0, concat_axis=0, tiled=True)
    return call(
        finish_kernel,
        [(count, count), (count, width), (count, width)],
        inverse,
        basis_new,
        image_start,
        image,
        start,
        parts,
        to_hbm=True,
        scratch=[
            pltpu.VMEM((count, count), jnp.float32),
            pltpu.VMEM((count, width), jnp.float32),
            pltpu.SemaphoreType.DMA((3,)),
        ],
    )


def solution(mesh):
    in_specs = (
        P(("row", "col"), None, None),
        P(("row", "col")),
        P(("row", "col")),
        P(None, ("col", "row")),
        P(None, ("col", "row")),
        P(None, ("col", "row")),
    )
    out_specs = (P(), P(None, ("col", "row")), P(None, ("col", "row")))
    return jax.shard_map(local, mesh=mesh, in_specs=in_specs, out_specs=out_specs, check_vma=False)
```

```python
import functools

import jax
import jax.numpy as jnp
from jax import lax
from jax.experimental import pallas as pl
from jax.experimental.pallas import tpu as pltpu
from jax.sharding import PartitionSpec as P

HIGHEST = lax.Precision.HIGHEST
LANES = 128
SUBLANES = 8
PANEL = 16
FLOPS_PER_US = 1.1e9
BYTES_PER_US = 3.6e6
VMEM_LIMIT = 32 * 1024 * 1024


def contract_last(left, right):
    return lax.dot_general(
        left,
        right,
        (((1,), (1,)), ((), ())),
        precision=HIGHEST,
        preferred_element_type=jnp.float32,
    )


def multiply(left, right):
    return jnp.dot(left, right, precision=HIGHEST, preferred_element_type=jnp.float32)


def pairwise(terms):
    while len(terms) > 1:
        terms = [sum(terms[i + 1 : i + 2], terms[i]) for i in range(0, len(terms), 2)]
    return terms[0]


def side_by_side(blocks_ref):
    return jnp.concatenate([blocks_ref[b] for b in range(blocks_ref.shape[0])], axis=1)


def load_kernel(
    trial_hbm, basis_hbm, image_hbm, rows_hbm, cols_hbm,
    wide_ref, basis_ref, image_ref, rows_ref, cols_ref, trial_vmem, basis_vmem, sems,
):
    copies = [
        pltpu.make_async_copy(source, target, sems.at[i])
        for i, (source, target) in enumerate(
            [
                (trial_hbm, trial_vmem),
                (basis_hbm, basis_vmem),
                (image_hbm, image_ref),
                (rows_hbm, rows_ref),
                (cols_hbm, cols_ref),
            ]
        )
    ]
    for copy in copies:
        copy.start()
    copies[0].wait()
    trial = trial_vmem[...].astype(jnp.float32)
    for b in range(wide_ref.shape[0]):
        wide_ref[b] = trial[:, b * LANES : (b + 1) * LANES]
    copies[1].wait()
    basis_ref[...] = jnp.concatenate([basis_vmem[...], trial], axis=0)
    for copy in copies[2:]:
        copy.wait()


def gram_kernel(scale, wide_ref, basis_ref, image_ref, sent_ref):
    blocks, vecs = wide_ref.shape[:2]
    basis_all = basis_ref[...]
    correlation = contract_last(basis_all, basis_all)
    coupling = contract_last(basis_all, image_ref[...])
    count = correlation.shape[0]
    unused = jnp.zeros((count, LANES - count - coupling.shape[1]), jnp.float32)
    gram = jnp.concatenate([correlation, coupling, unused], axis=1) * scale
    sent_ref[:blocks] = wide_ref[...]
    for i in range(sent_ref.shape[0] - blocks):
        sent_ref[blocks + i] = gram[i * vecs : (i + 1) * vecs]


def split(index, size):
    return index >> (size.bit_length() - 1), index & (size - 1)


def place(apart, bits):
    if bits == bits_of(1 << len(bits)):
        return apart
    return sum(((apart >> (m.bit_length() - 1)) & 1) << j for j, m in enumerate(bits))


def tiles_product(contract, by_rows, by_cols, n_row, blocks, scalars, tiles_ref, vecs_ref, sums_ref):
    position_ref, rows_ref, cols_ref = scalars
    sums_ref[...] = jnp.zeros_like(sums_ref)
    row, col = position_ref[0], position_ref[1]
    for t in range(tiles_ref.shape[0]):
        row_piece, row_inner = split(rows_ref[t], blocks)
        col_piece, col_inner = split(cols_ref[t] - col * (blocks * n_row), blocks)
        at_row = place(split(row_piece, n_row)[0] ^ col, by_rows) * blocks + row_inner
        at_col = place(col_piece ^ row, by_cols) * blocks + col_inner
        source, target = (at_col, at_row) if contract else (at_row, at_col)
        product = lax.dot_general(
            vecs_ref[source].astype(jnp.bfloat16),
            tiles_ref[t],
            (((1,), (contract,)), ((), ())),
            preferred_element_type=jnp.float32,
        )
        sums_ref[target] = sums_ref[target] + product


def backward_kernel(by_rows, by_cols, n_row, blocks, n_got, _, *refs):
    scalars, tiles_ref, own_ref = refs[:3], refs[3], refs[4]
    got_refs = refs[5 : 5 + n_got]
    kept_ref, sent_ref, vecs_ref, sums_ref = refs[5 + n_got :]
    for p, ref in enumerate([own_ref, *got_refs]):
        vecs_ref[p * blocks : (p + 1) * blocks] = ref[:blocks]
    tiles_product(0, by_rows, by_cols, n_row, blocks, scalars, tiles_ref, vecs_ref, sums_ref)
    half = kept_ref.shape[0]
    kept_ref[...] = sums_ref[:half]
    sent_ref[:half] = sums_ref[half:]
    sent_ref[half:] = pairwise([ref[blocks:] for ref in (own_ref, *got_refs)])


def forward_kernel(by_rows, by_cols, n_row, blocks, n_got, *refs):
    scalars, tiles_ref = refs[:3], refs[3]
    got_refs = refs[4 : 4 + n_got]
    *piece_refs, vecs_ref, sums_ref = refs[4 + n_got :]
    at = 0
    for ref in got_refs:
        vecs_ref[at : at + ref.shape[0]] = ref[...]
        at += ref.shape[0]
    tiles_product(1, by_rows, by_cols, n_row, blocks, scalars, tiles_ref, vecs_ref, sums_ref)
    for p, ref in enumerate(piece_refs):
        ref[...] = sums_ref[p * blocks : (p + 1) * blocks]


def fold_kernel(_, kept_ref, sent_ref, got_ref, kept_next_ref, sent_next_ref):
    size, half = kept_ref.shape[0], kept_next_ref.shape[0]
    kept_next_ref[...] = kept_ref[:half] + got_ref[:half]
    sent_next_ref[:half] = kept_ref[half:] + got_ref[half:size]
    sent_next_ref[half:] = sent_ref[size:] + got_ref[size:]


def factor_kernel(count, blocks, *refs):
    sent_ref, got_ref, inverse_ref, gram_ref = refs[-4:]
    summed = sent_ref[blocks:] + got_ref[blocks:]
    gram = jnp.concatenate([summed[i] for i in range(summed.shape[0])], axis=0)
    gram_ref[...] = gram
    row_id = lax.broadcasted_iota(jnp.int32, (count, LANES), 0)
    lane_id = lax.broadcasted_iota(jnp.int32, (count, LANES), 1)
    identity = jnp.where(lane_id == row_id + count, 1.0, 0.0)
    work = jnp.where(lane_id < count, gram, identity)
    tiles = count // SUBLANES
    work = [work[SUBLANES * g : SUBLANES * (g + 1)] for g in range(tiles)]
    sublane = lax.broadcasted_iota(jnp.int32, (SUBLANES, LANES), 0)
    diagonal = [jnp.ones((SUBLANES, LANES), jnp.float32)] * tiles

    def spread(tile, i):
        return jnp.broadcast_to(tile[i : i + 1, :], (SUBLANES, LANES))

    for start in range(0, count, PANEL):
        stop = min(start + PANEL, count)
        first = start // SUBLANES
        columns = {
            j: {
                g: jnp.broadcast_to(work[g][:, j : j + 1], (SUBLANES, LANES))
                for g in range(first, tiles)
            }
            for j in range(start, stop)
        }
        for j in range(start, stop):
            i, own = j % SUBLANES, j // SUBLANES
            pivot = spread(columns[j][own], i)
            diagonal[own] = jnp.where(sublane == i, pivot, diagonal[own])
            reciprocal = 1.0 / pivot
            row = spread(work[own], i)
            entries = {k: spread(columns[k][own], i) for k in range(j + 1, stop)}
            for g in range(own, tiles):
                ratio = columns[j][g] * reciprocal
                if g == own:
                    ratio = jnp.where(sublane > i, ratio, 0.0)
                work[g] = work[g] - ratio * row
                for k in range(j + 1, stop):
                    columns[k][g] = columns[k][g] - ratio * entries[k]
    for g in range(tiles):
        scaled = work[g] * lax.rsqrt(diagonal[g])
        inverse_ref[SUBLANES * g : SUBLANES * (g + 1), :] = scaled[:, count : 2 * count]


def basis_kernel(inverse_ref, gram_ref, basis_ref, image_ref, basis_new_ref, image_start_ref, start_ref):
    inverse = inverse_ref[...]
    count, old = inverse.shape[0], image_ref.shape[0]
    basis_new_ref[...] = multiply(inverse, basis_ref[...])
    image_start_ref[...] = multiply(inverse[:, :old], image_ref[...])
    coupling = gram_ref[:, count : count + old]
    start_ref[...] = contract_last(multiply(inverse, coupling), inverse[:, :old])


def image_kernel(scale, basis_new_ref, *refs):
    *sums_refs, image_ref, part_ref = refs
    blocks = sums_refs[0].shape[0]
    summed = pairwise([ref[:blocks] for ref in sums_refs])
    image = jnp.concatenate([summed[b] for b in range(summed.shape[0])], axis=1)
    image_ref[...] = image
    vecs, count = image.shape[0], basis_new_ref.shape[0]
    part = contract_last(image, basis_new_ref[...]) * scale
    part = jnp.concatenate([part, jnp.zeros((vecs, LANES - count), jnp.float32)], axis=1)
    part_ref[...] = jnp.broadcast_to(part[None], part_ref.shape)


def finish_kernel(
    inverse_ref, basis_new_ref, image_start_ref, image_ref, start_ref, parts_ref,
    projected_hbm, basis_new_hbm, image_new_hbm, projected_vmem, image_new_vmem, sems,
):
    basis_copy = pltpu.make_async_copy(basis_new_ref, basis_new_hbm, sems.at[0])
    basis_copy.start()
    vecs = image_ref.shape[0]
    count = inverse_ref.shape[0]
    last = inverse_ref[...][:, count - vecs :]
    image_new_vmem[...] = image_start_ref[...] + multiply(last, image_ref[...])
    image_copy = pltpu.make_async_copy(image_new_vmem, image_new_hbm, sems.at[1])
    image_copy.start()
    total = jnp.sum(parts_ref[...], axis=0)
    new = lax.dot_general(
        total[:, :count],
        last,
        (((0,), (1,)), ((), ())),
        precision=HIGHEST,
        preferred_element_type=jnp.float32,
    )
    projected_vmem[...] = start_ref[...] + new
    projected_copy = pltpu.make_async_copy(projected_vmem, projected_hbm, sems.at[2])
    projected_copy.start()
    basis_copy.wait()
    image_copy.wait()
    projected_copy.wait()


def call(kernel, outs, *args, time=0.0, after=0, smem=0, from_hbm=False, to_hbm=False, scratch=()):
    operand = pl.BlockSpec(memory_space=pltpu.HBM if from_hbm else pltpu.VMEM)
    result = pl.BlockSpec(memory_space=pltpu.HBM if to_hbm else pltpu.VMEM)
    scalars = pl.BlockSpec(memory_space=pltpu.SMEM)
    if from_hbm:
        args = [pltpu.with_memory_space_constraint(arg, pltpu.HBM) for arg in args]
    outs = [o if hasattr(o, "dtype") else jax.ShapeDtypeStruct(o, jnp.float32) for o in outs]
    return pl.pallas_call(
        kernel,
        out_shape=outs,
        in_specs=[operand] * after + [scalars] * smem + [operand] * (len(args) - smem - after),
        out_specs=[result] * len(outs),
        scratch_shapes=scratch,
        compiler_params=pltpu.CompilerParams(vmem_limit_bytes=VMEM_LIMIT),
        cost_estimate=pl.CostEstimate(
            flops=int(time * FLOPS_PER_US), bytes_accessed=int(time * BYTES_PER_US), transcendentals=0
        ),
    )(*args)


def bits_of(size):
    return [1 << j for j in range(size.bit_length() - 1)]


def swap(array, axis, mask):
    size = lax.axis_size(axis)
    return lax.ppermute(array, axis, [(i, i ^ mask) for i in range(size)])


def local(tile_blocks, tile_rows, tile_cols, trial_vectors, basis_old, image_old):
    tile_size = tile_blocks.shape[1]
    vecs, width = trial_vectors.shape
    old = basis_old.shape[0]
    count = old + vecs
    blocks = width // tile_size
    n_row, n_col = lax.axis_size("row"), lax.axis_size("col")
    row, col = lax.axis_index("row"), lax.axis_index("col")
    scale = 1.0 / float(width * n_row * n_col)
    row_bits, col_bits = bits_of(n_row), bits_of(n_col)
    gather_row = row_bits[1:] + row_bits[:1]
    scatter_row = row_bits
    grams = count // vecs
    position = jnp.stack([row, col])

    places = jax.ShapeDtypeStruct(tile_rows.shape, tile_rows.dtype)
    wide, basis_all, image_kept, rows_kept, cols_kept = call(
        load_kernel,
        [(blocks, vecs, tile_size), (count, width), (old, width), places, places],
        trial_vectors,
        basis_old,
        image_old,
        tile_rows,
        tile_cols,
        time=0.0,
        from_hbm=True,
        scratch=[
            pltpu.VMEM((vecs, width), trial_vectors.dtype),
            pltpu.VMEM((old, width), jnp.float32),
            pltpu.SemaphoreType.DMA((5,)),
        ],
    )
    col_got, payloads = [wide], []
    for m in gather_row:
        payloads.append(jnp.concatenate(col_got, axis=0))
        col_got.append(swap(payloads[-1], "row", m))
    (own,) = call(
        functools.partial(gram_kernel, scale),
        [(blocks + grams, vecs, LANES)],
        wide,
        basis_all,
        image_kept,
    )
    row_got = [swap(own, "col", m) for m in range(1, n_col)]

    half = blocks * n_row // 2
    kept, sent = call(
        functools.partial(
            backward_kernel, col_bits, scatter_row[::-1], n_row, blocks, len(row_got)
        ),
        [(half, vecs, tile_size), (half + grams, vecs, tile_size)],
        payloads[1],
        position,
        rows_kept,
        cols_kept,
        tile_blocks,
        own,
        *row_got,
        after=1,
        smem=3,
        scratch=[
            pltpu.VMEM((blocks * n_col, vecs, tile_size), jnp.float32),
            pltpu.VMEM((blocks * n_row, vecs, tile_size), jnp.float32),
        ],
    )
    forward = call(
        functools.partial(forward_kernel, col_bits, gather_row, n_row, blocks, len(col_got)),
        [(blocks, vecs, tile_size)] * n_col,
        position,
        rows_kept,
        cols_kept,
        tile_blocks,
        *col_got,
        smem=3,
        scratch=[
            pltpu.VMEM((blocks * n_row, vecs, tile_size), jnp.float32),
            pltpu.VMEM((blocks * n_col, vecs, tile_size), jnp.float32),
        ],
    )
    row_parts = [forward[0]] + [swap(part, "col", m) for m, part in enumerate(forward) if m]
    for m in scatter_row[:-1]:
        half //= 2
        kept, sent = call(
            fold_kernel,
            [(half, vecs, tile_size), (half + grams, vecs, tile_size)],
            forward[0] if m == scatter_row[-2] else wide,
            kept,
            sent,
            swap(sent, "row", m),
        )
    got = swap(sent, "row", scatter_row[-1])
    col_parts = [kept, got]

    inverse, gram = call(
        functools.partial(factor_kernel, count, blocks),
        [(count, count), (count, LANES)],
        row_parts[-1],
        sent,
        got,
        time=1.1,
    )
    basis_new, image_start, start = call(
        basis_kernel,
        [(count, width), (count, width), (count, count)],
        inverse,
        gram,
        basis_all,
        image_kept,
        time=0.7,
    )
    image, part = call(
        functools.partial(image_kernel, scale),
        [(vecs, width), (n_row * n_col, vecs, LANES)],
        basis_new,
        *row_parts,
        *col_parts,
        time=0.0,
    )
    parts = lax.all_to_all(part, ("row", "col"), split_axis=0, concat_axis=0, tiled=True)
    return call(
        finish_kernel,
        [(count, count), (count, width), (count, width)],
        inverse,
        basis_new,
        image_start,
        image,
        start,
        parts,
        to_hbm=True,
        scratch=[
            pltpu.VMEM((count, count), jnp.float32),
            pltpu.VMEM((count, width), jnp.float32),
            pltpu.SemaphoreType.DMA((3,)),
        ],
    )


def solution(mesh):
    in_specs = (
        P(("row", "col"), None, None),
        P(("row", "col")),
        P(("row", "col")),
        P(None, ("col", "row")),
        P(None, ("col", "row")),
        P(None, ("col", "row")),
    )
    out_specs = (P(), P(None, ("col", "row")), P(None, ("col", "row")))
    return jax.shard_map(local, mesh=mesh, in_specs=in_specs, out_specs=out_specs, check_vma=False)
```

```python
import functools

import jax
import jax.numpy as jnp
from jax import lax
from jax.experimental import pallas as pl
from jax.experimental.pallas import tpu as pltpu
from jax.sharding import PartitionSpec as P

HIGHEST = lax.Precision.HIGHEST
LANES = 128
SUBLANES = 8
PANEL = 16
GROUP = 2
FLOPS_PER_US = 1.1e9
BYTES_PER_US = 3.6e6
VMEM_LIMIT = 32 * 1024 * 1024


def three_parts(wide):
    high = wide.astype(jnp.bfloat16)
    rest = wide - high.astype(jnp.float32)
    middle = rest.astype(jnp.bfloat16)
    return high, middle, (rest - middle.astype(jnp.float32)).astype(jnp.bfloat16)


def product(left, right, contract):
    rows = left.shape[0]
    padding = -rows % 16
    if padding:
        left = jnp.concatenate([left, jnp.zeros((padding, left.shape[1]), left.dtype)], axis=0)
    size = rows + padding
    high, middle, low = three_parts(left)
    stacked = jnp.concatenate([high, middle, low], axis=0)
    sums = [
        lax.dot_general(
            stacked[: size * (3 - i)],
            part,
            (((1,), (contract,)), ((), ())),
            preferred_element_type=jnp.float32,
        )
        for i, part in enumerate(three_parts(right))
    ]
    small = (sums[0][2 * size : 2 * size + rows] + sums[1][size : size + rows]) + sums[2][:rows]
    middle = sums[0][size : size + rows] + sums[1][:rows]
    return sums[0][:rows] + (middle + small)


def contract_last(left, right):
    return product(left, right, 1)


def multiply(left, right):
    return product(left, right, 0)


def pairwise(terms):
    while len(terms) > 1:
        terms = [sum(terms[i + 1 : i + 2], terms[i]) for i in range(0, len(terms), 2)]
    return terms[0]


def side_by_side(blocks_ref):
    return jnp.concatenate([blocks_ref[b] for b in range(blocks_ref.shape[0])], axis=1)


def load_kernel(
    trial_hbm, basis_hbm, image_hbm, rows_hbm, cols_hbm,
    wide_ref, basis_ref, image_ref, rows_ref, cols_ref, trial_vmem, basis_vmem, sems,
):
    copies = [
        pltpu.make_async_copy(source, target, sems.at[i])
        for i, (source, target) in enumerate(
            [
                (trial_hbm, trial_vmem),
                (basis_hbm, basis_vmem),
                (image_hbm, image_ref),
                (rows_hbm, rows_ref),
                (cols_hbm, cols_ref),
            ]
        )
    ]
    for copy in copies:
        copy.start()
    copies[0].wait()
    trial = trial_vmem[...].astype(jnp.float32)
    for b in range(wide_ref.shape[0]):
        wide_ref[b] = trial[:, b * LANES : (b + 1) * LANES]
    copies[1].wait()
    basis_ref[...] = jnp.concatenate([basis_vmem[...], trial], axis=0)
    for copy in copies[2:]:
        copy.wait()


def gram_kernel(scale, wide_ref, basis_ref, image_ref, sent_ref):
    blocks, vecs = wide_ref.shape[:2]
    basis_all = basis_ref[...]
    images = image_ref[...]
    unused = LANES - basis_all.shape[0] - images.shape[0]
    filler = jnp.zeros((unused, images.shape[1]), jnp.float32)
    gram = contract_last(basis_all, jnp.concatenate([basis_all, images, filler], axis=0)) * scale
    sent_ref[:blocks] = wide_ref[...]
    for i in range(sent_ref.shape[0] - blocks):
        sent_ref[blocks + i] = gram[i * vecs : (i + 1) * vecs]


def split(index, size):
    return index >> (size.bit_length() - 1), index & (size - 1)


def place(apart, bits):
    if bits == bits_of(1 << len(bits)):
        return apart
    return sum(((apart >> (m.bit_length() - 1)) & 1) << j for j, m in enumerate(bits))


def tiles_product(contract, by_rows, by_cols, n_row, blocks, scalars, tiles_ref, vecs_ref, sums_ref):
    rows_ref, cols_ref = scalars
    sums_ref[...] = jnp.zeros_like(sums_ref)
    row, col = lax.axis_index("row"), lax.axis_index("col")
    places = []
    for t in range(tiles_ref.shape[0]):
        row_piece, row_inner = split(rows_ref[t], blocks)
        col_piece, col_inner = split(cols_ref[t] - col * (blocks * n_row), blocks)
        at_row = place(split(row_piece, n_row)[0] ^ col, by_rows) * blocks + row_inner
        at_col = place(col_piece ^ row, by_cols) * blocks + col_inner
        places.append((at_col, at_row) if contract else (at_row, at_col))
    vecs, size = vecs_ref.shape[1:]
    for t in range(0, len(places), GROUP):
        group = range(t, min(t + GROUP, len(places)))
        picked = jnp.concatenate([vecs_ref[places[u][0]] for u in group], axis=0)
        products = lax.dot_general(
            picked.astype(jnp.bfloat16),
            jnp.concatenate([tiles_ref[u] for u in group], axis=1 - contract),
            (((1,), (contract,)), ((), ())),
            preferred_element_type=jnp.float32,
        )
        for i, u in enumerate(group):
            target = places[u][1]
            own = products[i * vecs : (i + 1) * vecs, i * size : (i + 1) * size]
            sums_ref[target] = sums_ref[target] + own


def backward_kernel(by_rows, by_cols, n_row, blocks, n_got, *refs):
    scalars, tiles_ref, own_ref = refs[:2], refs[2], refs[3]
    got_refs = refs[4 : 4 + n_got]
    kept_ref, sent_ref, vecs_ref, sums_ref = refs[4 + n_got :]
    for p, ref in enumerate([own_ref, *got_refs]):
        vecs_ref[p * blocks : (p + 1) * blocks] = ref[:blocks]
    tiles_product(0, by_rows, by_cols, n_row, blocks, scalars, tiles_ref, vecs_ref, sums_ref)
    half = kept_ref.shape[0]
    kept_ref[...] = sums_ref[:half]
    sent_ref[:half] = sums_ref[half:]
    sent_ref[half:] = pairwise([ref[blocks:] for ref in (own_ref, *got_refs)])


def forward_kernel(by_rows, by_cols, n_row, blocks, n_got, *refs):
    scalars, tiles_ref = refs[:2], refs[2]
    got_refs = refs[3 : 3 + n_got]
    *piece_refs, vecs_ref, sums_ref = refs[3 + n_got :]
    at = 0
    for ref in got_refs:
        vecs_ref[at : at + ref.shape[0]] = ref[...]
        at += ref.shape[0]
    tiles_product(1, by_rows, by_cols, n_row, blocks, scalars, tiles_ref, vecs_ref, sums_ref)
    at = 0
    for ref in piece_refs:
        ref[...] = sums_ref[at : at + ref.shape[0]]
        at += ref.shape[0]


def fold_kernel(kept_ref, sent_ref, got_ref, kept_next_ref, sent_next_ref):
    size, half = kept_ref.shape[0], kept_next_ref.shape[0]
    kept_next_ref[...] = kept_ref[:half] + got_ref[:half]
    sent_next_ref[:half] = kept_ref[half:] + got_ref[half:size]
    if sent_next_ref.shape[0] > half:
        sent_next_ref[half:] = sent_ref[size:] + got_ref[size:]


def factor_kernel(count, blocks, sent_ref, got_ref, inverse_ref, gram_ref):
    summed = sent_ref[blocks:] + got_ref[blocks:]
    gram = jnp.concatenate([summed[i] for i in range(summed.shape[0])], axis=0)
    gram_ref[...] = gram
    row_id = lax.broadcasted_iota(jnp.int32, (count, LANES), 0)
    lane_id = lax.broadcasted_iota(jnp.int32, (count, LANES), 1)
    identity = jnp.where(lane_id == row_id + count, 1.0, 0.0)
    work = jnp.where(lane_id < count, gram, identity)
    tiles = count // SUBLANES
    work = [work[SUBLANES * g : SUBLANES * (g + 1)] for g in range(tiles)]
    sublane = lax.broadcasted_iota(jnp.int32, (SUBLANES, LANES), 0)
    diagonal = [jnp.ones((SUBLANES, LANES), jnp.float32)] * tiles

    def spread(tile, i):
        return jnp.broadcast_to(tile[i : i + 1, :], (SUBLANES, LANES))

    for start in range(0, count, PANEL):
        stop = min(start + PANEL, count)
        first = start // SUBLANES
        columns = {
            j: {
                g: jnp.broadcast_to(work[g][:, j : j + 1], (SUBLANES, LANES))
                for g in range(first, tiles)
            }
            for j in range(start, stop)
        }
        for j in range(start, stop):
            i, own = j % SUBLANES, j // SUBLANES
            pivot = spread(columns[j][own], i)
            diagonal[own] = jnp.where(sublane == i, pivot, diagonal[own])
            reciprocal = 1.0 / pivot
            row = spread(work[own], i)
            entries = {k: spread(columns[k][own], i) for k in range(j + 1, stop)}
            for g in range(own, tiles):
                ratio = columns[j][g] * reciprocal
                if g == own:
                    ratio = jnp.where(sublane > i, ratio, 0.0)
                work[g] = work[g] - ratio * row
                for k in range(j + 1, stop):
                    columns[k][g] = columns[k][g] - ratio * entries[k]
    for g in range(tiles):
        scaled = work[g] * lax.rsqrt(diagonal[g])
        inverse_ref[SUBLANES * g : SUBLANES * (g + 1), :] = scaled[:, count : 2 * count]


def basis_kernel(inverse_ref, gram_ref, basis_ref, image_ref, basis_new_ref, image_start_ref, start_ref):
    inverse = inverse_ref[...]
    count, old = inverse.shape[0], image_ref.shape[0]
    basis_new_ref[...] = multiply(inverse, basis_ref[...])
    image_start_ref[...] = multiply(inverse[:, :old], image_ref[...])
    coupling = gram_ref[:, count : count + old]
    start_ref[...] = contract_last(multiply(inverse, coupling), inverse[:, :old])


def image_kernel(scale, basis_new_ref, *refs):
    *sums_refs, image_ref, part_ref = refs
    blocks = sums_refs[0].shape[0]
    summed = pairwise([ref[:blocks] for ref in sums_refs])
    image = jnp.concatenate([summed[b] for b in range(summed.shape[0])], axis=1)
    image_ref[...] = image
    vecs, count = image.shape[0], basis_new_ref.shape[0]
    part = contract_last(image, basis_new_ref[...]) * scale
    part = jnp.concatenate([part, jnp.zeros((vecs, LANES - count), jnp.float32)], axis=1)
    part_ref[...] = jnp.broadcast_to(part[None], part_ref.shape)


def finish_kernel(
    inverse_ref, basis_new_ref, image_start_ref, image_ref, start_ref, parts_ref,
    projected_hbm, basis_new_hbm, image_new_hbm, projected_vmem, image_new_vmem, sems,
):
    basis_copy = pltpu.make_async_copy(basis_new_ref, basis_new_hbm, sems.at[0])
    basis_copy.start()
    vecs = image_ref.shape[0]
    count = inverse_ref.shape[0]
    last = inverse_ref[...][:, count - vecs :]
    image_new = image_start_ref[...]
    for k in range(vecs):
        image_new = image_new + last[:, k : k + 1] * image_ref[k : k + 1, :]
    image_new_vmem[...] = image_new
    image_copy = pltpu.make_async_copy(image_new_vmem, image_new_hbm, sems.at[1])
    image_copy.start()
    total = jnp.sum(parts_ref[...], axis=0)
    new = lax.dot_general(
        total[:, :count],
        last,
        (((0,), (1,)), ((), ())),
        precision=HIGHEST,
        preferred_element_type=jnp.float32,
    )
    projected_vmem[...] = start_ref[...] + new
    projected_copy = pltpu.make_async_copy(projected_vmem, projected_hbm, sems.at[2])
    projected_copy.start()
    basis_copy.wait()
    image_copy.wait()
    projected_copy.wait()


def call(kernel, outs, *args, after=(), time=0.0, smem=0, from_hbm=False, to_hbm=False, scratch=()):
    operand = pl.BlockSpec(memory_space=pltpu.HBM if from_hbm else pltpu.VMEM)
    result = pl.BlockSpec(memory_space=pltpu.HBM if to_hbm else pltpu.VMEM)
    scalars = pl.BlockSpec(memory_space=pltpu.SMEM)
    if from_hbm:
        args = [pltpu.with_memory_space_constraint(arg, pltpu.HBM) for arg in args]
    result_specs = [scalars if hasattr(o, "dtype") else result for o in outs]
    outs = [o if hasattr(o, "dtype") else jax.ShapeDtypeStruct(o, jnp.float32) for o in outs]
    n_after = len(after)

    def body(*refs):
        kernel(*refs[n_after:])

    return pl.pallas_call(
        body,
        out_shape=outs,
        in_specs=[operand] * n_after + [scalars] * smem + [operand] * (len(args) - smem),
        out_specs=result_specs,
        scratch_shapes=scratch,
        compiler_params=pltpu.CompilerParams(vmem_limit_bytes=VMEM_LIMIT),
        cost_estimate=pl.CostEstimate(
            flops=int(time * FLOPS_PER_US), bytes_accessed=int(time * BYTES_PER_US), transcendentals=0
        ),
        name=(kernel.func if hasattr(kernel, "func") else kernel).__name__[:-7],
    )(*after, *args)


def bits_of(size):
    return [1 << j for j in range(size.bit_length() - 1)]


def swap(array, axis, mask):
    size = lax.axis_size(axis)
    return lax.ppermute(array, axis, [(i, i ^ mask) for i in range(size)])


def local(tile_blocks, tile_rows, tile_cols, trial_vectors, basis_old, image_old):
    tile_size = tile_blocks.shape[1]
    vecs, width = trial_vectors.shape
    old = basis_old.shape[0]
    count = old + vecs
    blocks = width // tile_size
    n_row, n_col = lax.axis_size("row"), lax.axis_size("col")
    scale = 1.0 / float(width * n_row * n_col)
    row_bits, col_bits = bits_of(n_row), bits_of(n_col)
    gather_row = row_bits[1:] + row_bits[:1]
    scatter_row, scatter_col = row_bits, col_bits
    grams = count // vecs
    tile = (vecs, tile_size)

    places = pltpu.SMEM(tile_rows.shape, tile_rows.dtype)
    wide, basis_all, image_kept, rows_kept, cols_kept = call(
        load_kernel,
        [(blocks, *tile), (count, width), (old, width), places, places],
        trial_vectors,
        basis_old,
        image_old,
        tile_rows,
        tile_cols,
        time=1.0,
        from_hbm=True,
        scratch=[
            pltpu.VMEM((vecs, width), trial_vectors.dtype),
            pltpu.VMEM((old, width), jnp.float32),
            pltpu.SemaphoreType.DMA((5,)),
        ],
    )
    (own,) = call(
        functools.partial(gram_kernel, scale),
        [(blocks + grams, *tile)],
        wide,
        basis_all,
        image_kept,
        time=0.5,
    )
    row_got = [swap(own, "col", m) for m in range(1, n_col)]
    col_got = [wide]
    for m in gather_row:
        col_got.append(swap(jnp.concatenate(col_got, axis=0), "row", m))

    half_row, half_col = blocks * n_row // 2, blocks * n_col // 2
    col_kept, col_sent = call(
        functools.partial(
            backward_kernel, col_bits, scatter_row[::-1], n_row, blocks, len(row_got)
        ),
        [(half_row, *tile), (half_row + grams, *tile)],
        rows_kept,
        cols_kept,
        tile_blocks,
        own,
        *row_got,
        time=1.0,
        smem=2,
        scratch=[
            pltpu.VMEM((2 * half_col, *tile), jnp.float32),
            pltpu.VMEM((2 * half_row, *tile), jnp.float32),
        ],
    )
    row_kept, row_sent = call(
        functools.partial(
            forward_kernel, scatter_col[::-1], gather_row, n_row, blocks, len(col_got)
        ),
        [(half_col, *tile)] * 2,
        rows_kept,
        cols_kept,
        tile_blocks,
        *col_got,
        time=1.0,
        smem=2,
        scratch=[
            pltpu.VMEM((2 * half_row, *tile), jnp.float32),
            pltpu.VMEM((2 * half_col, *tile), jnp.float32),
        ],
    )
    forward_done = row_kept
    for i, m in enumerate(scatter_row[:-1]):
        half_row //= 2
        col_kept, col_sent = call(
            fold_kernel,
            [(half_row, *tile), (half_row + grams, *tile)],
            col_kept,
            col_sent,
            swap(col_sent, "row", m),
            after=[forward_done] if i == n_row.bit_length() - 3 else [],
            time=0.1,
        )
    col_parts = [col_kept, swap(col_sent, "row", scatter_row[-1])]
    for m in scatter_col[:-1]:
        half_col //= 2
        row_kept, row_sent = call(
            fold_kernel,
            [(half_col, *tile)] * 2,
            row_kept,
            row_sent,
            swap(row_sent, "col", m),
            time=0.1,
        )
    row_parts = [row_kept, swap(row_sent, "col", scatter_col[-1])]

    inverse, gram = call(
        functools.partial(factor_kernel, count, blocks),
        [(count, count), (count, LANES)],
        col_sent,
        col_parts[1],
        time=1.1,
    )
    basis_new, image_start, start = call(
        basis_kernel,
        [(count, width), (count, width), (count, count)],
        inverse,
        gram,
        basis_all,
        image_kept,
    )
    image, part = call(
        functools.partial(image_kernel, scale),
        [(vecs, width), (n_row * n_col, vecs, LANES)],
        basis_new,
        *row_parts,
        *col_parts,
    )
    parts = lax.all_to_all(part, ("row", "col"), split_axis=0, concat_axis=0, tiled=True)
    return call(
        finish_kernel,
        [(count, count), (count, width), (count, width)],
        inverse,
        basis_new,
        image_start,
        image,
        start,
        parts,
        to_hbm=True,
        scratch=[
            pltpu.VMEM((count, count), jnp.float32),
            pltpu.VMEM((count, width), jnp.float32),
            pltpu.SemaphoreType.DMA((3,)),
        ],
    )


def solution(mesh):
    in_specs = (
        P(("row", "col"), None, None),
        P(("row", "col")),
        P(("row", "col")),
        P(None, ("col", "row")),
        P(None, ("col", "row")),
        P(None, ("col", "row")),
    )
    out_specs = (P(), P(None, ("col", "row")), P(None, ("col", "row")))
    return jax.shard_map(local, mesh=mesh, in_specs=in_specs, out_specs=out_specs, check_vma=False)
```

```python
import functools

import jax
import jax.numpy as jnp
from jax import lax
from jax.experimental import pallas as pl
from jax.experimental.pallas import tpu as pltpu
from jax.sharding import PartitionSpec as P

HIGHEST = lax.Precision.HIGHEST
LANES = 128
SUBLANES = 8
PANEL = 16
GROUP = 2
FLOPS_PER_US = 1.1e9
BYTES_PER_US = 3.6e6
VMEM_LIMIT = 32 * 1024 * 1024


def three_parts(wide):
    high = wide.astype(jnp.bfloat16)
    rest = wide - high.astype(jnp.float32)
    middle = rest.astype(jnp.bfloat16)
    return high, middle, (rest - middle.astype(jnp.float32)).astype(jnp.bfloat16)


def product(left, right, contract):
    rows = left.shape[0]
    padding = -rows % 16
    if padding:
        left = jnp.concatenate([left, jnp.zeros((padding, left.shape[1]), left.dtype)], axis=0)
    size = rows + padding
    high, middle, low = three_parts(left)
    stacked = jnp.concatenate([high, middle, low], axis=0)
    sums = [
        lax.dot_general(
            stacked[: size * (3 - i)],
            part,
            (((1,), (contract,)), ((), ())),
            preferred_element_type=jnp.float32,
        )
        for i, part in enumerate(three_parts(right))
    ]
    small = (sums[0][2 * size : 2 * size + rows] + sums[1][size : size + rows]) + sums[2][:rows]
    middle = sums[0][size : size + rows] + sums[1][:rows]
    return sums[0][:rows] + (middle + small)


def contract_last(left, right):
    return product(left, right, 1)


def multiply(left, right):
    return product(left, right, 0)


def pairwise(terms):
    while len(terms) > 1:
        terms = [sum(terms[i + 1 : i + 2], terms[i]) for i in range(0, len(terms), 2)]
    return terms[0]


def side_by_side(blocks_ref):
    return jnp.concatenate([blocks_ref[b] for b in range(blocks_ref.shape[0])], axis=1)


def load_kernel(
    trial_hbm, basis_hbm, image_hbm, rows_hbm, cols_hbm,
    wide_ref, basis_ref, image_ref, rows_ref, cols_ref, trial_vmem, basis_vmem, sems,
):
    copies = [
        pltpu.make_async_copy(source, target, sems.at[i])
        for i, (source, target) in enumerate(
            [
                (trial_hbm, trial_vmem),
                (basis_hbm, basis_vmem),
                (image_hbm, image_ref),
                (rows_hbm, rows_ref),
                (cols_hbm, cols_ref),
            ]
        )
    ]
    for copy in copies:
        copy.start()
    copies[0].wait()
    trial = trial_vmem[...].astype(jnp.float32)
    for b in range(wide_ref.shape[0]):
        wide_ref[b] = trial[:, b * LANES : (b + 1) * LANES]
    copies[1].wait()
    basis_ref[...] = jnp.concatenate([basis_vmem[...], trial], axis=0)
    for copy in copies[2:]:
        copy.wait()


def gram_kernel(scale, wide_ref, basis_ref, image_ref, sent_ref):
    blocks, vecs = wide_ref.shape[:2]
    basis_all = basis_ref[...]
    images = image_ref[...]
    unused = LANES - basis_all.shape[0] - images.shape[0]
    filler = jnp.zeros((unused, images.shape[1]), jnp.float32)
    gram = contract_last(basis_all, jnp.concatenate([basis_all, images, filler], axis=0)) * scale
    sent_ref[:blocks] = wide_ref[...]
    for i in range(sent_ref.shape[0] - blocks):
        sent_ref[blocks + i] = gram[i * vecs : (i + 1) * vecs]


def split(index, size):
    return index >> (size.bit_length() - 1), index & (size - 1)


def place(apart, masks):
    crossed = any(m & (m - 1) for m in masks)
    at = 0
    for j, m in enumerate(masks):
        bit = apart >> (m.bit_length() - 1)
        if m == 1 and crossed:
            for k in range(1, len(masks)):
                bit = bit ^ (apart >> k)
        at = at + ((bit & 1) << j)
    return at


def tiles_product(contract, by_rows, by_cols, n_row, blocks, scalars, tiles_ref, vecs_ref, sums_ref):
    rows_ref, cols_ref = scalars
    sums_ref[...] = jnp.zeros_like(sums_ref)
    row, col = lax.axis_index("row"), lax.axis_index("col")
    places = []
    for t in range(tiles_ref.shape[0]):
        row_piece, row_inner = split(rows_ref[t], blocks)
        col_piece, col_inner = split(cols_ref[t] - col * (blocks * n_row), blocks)
        at_row = place(split(row_piece, n_row)[0] ^ col, by_rows) * blocks + row_inner
        at_col = place(col_piece ^ row, by_cols) * blocks + col_inner
        places.append((at_col, at_row) if contract else (at_row, at_col))
    vecs, size = vecs_ref.shape[1:]
    for t in range(0, len(places), GROUP):
        group = range(t, min(t + GROUP, len(places)))
        picked = jnp.concatenate([vecs_ref[places[u][0]] for u in group], axis=0)
        products = lax.dot_general(
            picked.astype(jnp.bfloat16),
            jnp.concatenate([tiles_ref[u] for u in group], axis=1 - contract),
            (((1,), (contract,)), ((), ())),
            preferred_element_type=jnp.float32,
        )
        for i, u in enumerate(group):
            target = places[u][1]
            own = products[i * vecs : (i + 1) * vecs, i * size : (i + 1) * size]
            sums_ref[target] = sums_ref[target] + own


def backward_kernel(by_rows, by_cols, n_row, blocks, n_got, *refs):
    scalars, tiles_ref, own_ref = refs[:2], refs[2], refs[3]
    got_refs = refs[4 : 4 + n_got]
    kept_ref, sent_ref, vecs_ref, sums_ref = refs[4 + n_got :]
    for p, ref in enumerate([own_ref, *got_refs]):
        vecs_ref[p * blocks : (p + 1) * blocks] = ref[:blocks]
    tiles_product(0, by_rows, by_cols, n_row, blocks, scalars, tiles_ref, vecs_ref, sums_ref)
    half = kept_ref.shape[0]
    kept_ref[...] = sums_ref[:half]
    sent_ref[:half] = sums_ref[half:]
    sent_ref[half:] = pairwise([ref[blocks:] for ref in (own_ref, *got_refs)])


def forward_kernel(by_rows, by_cols, n_row, blocks, n_got, *refs):
    scalars, tiles_ref = refs[:2], refs[2]
    got_refs = refs[3 : 3 + n_got]
    *piece_refs, vecs_ref, sums_ref = refs[3 + n_got :]
    at = 0
    for ref in got_refs:
        vecs_ref[at : at + ref.shape[0]] = ref[...]
        at += ref.shape[0]
    tiles_product(1, by_rows, by_cols, n_row, blocks, scalars, tiles_ref, vecs_ref, sums_ref)
    at = 0
    for ref in piece_refs:
        ref[...] = sums_ref[at : at + ref.shape[0]]
        at += ref.shape[0]


def fold_kernel(kept_ref, sent_ref, got_ref, kept_next_ref, sent_next_ref):
    size, half = kept_ref.shape[0], kept_next_ref.shape[0]
    kept_next_ref[...] = kept_ref[:half] + got_ref[:half]
    sent_next_ref[:half] = kept_ref[half:] + got_ref[half:size]
    if sent_next_ref.shape[0] > half:
        sent_next_ref[half:] = sent_ref[size:] + got_ref[size:]


def factor_kernel(count, blocks, sent_ref, got_ref, inverse_ref, gram_ref):
    summed = sent_ref[blocks:] + got_ref[blocks:]
    gram = jnp.concatenate([summed[i] for i in range(summed.shape[0])], axis=0)
    gram_ref[...] = gram
    row_id = lax.broadcasted_iota(jnp.int32, (count, LANES), 0)
    lane_id = lax.broadcasted_iota(jnp.int32, (count, LANES), 1)
    identity = jnp.where(lane_id == row_id + count, 1.0, 0.0)
    work = jnp.where(lane_id < count, gram, identity)
    tiles = count // SUBLANES
    work = [work[SUBLANES * g : SUBLANES * (g + 1)] for g in range(tiles)]
    sublane = lax.broadcasted_iota(jnp.int32, (SUBLANES, LANES), 0)
    diagonal = [jnp.ones((SUBLANES, LANES), jnp.float32)] * tiles

    def spread(tile, i):
        return jnp.broadcast_to(tile[i : i + 1, :], (SUBLANES, LANES))

    for start in range(0, count, PANEL):
        stop = min(start + PANEL, count)
        first = start // SUBLANES
        columns = {
            j: {
                g: jnp.broadcast_to(work[g][:, j : j + 1], (SUBLANES, LANES))
                for g in range(first, tiles)
            }
            for j in range(start, stop)
        }
        for j in range(start, stop):
            i, own = j % SUBLANES, j // SUBLANES
            pivot = spread(columns[j][own], i)
            diagonal[own] = jnp.where(sublane == i, pivot, diagonal[own])
            reciprocal = 1.0 / pivot
            row = spread(work[own], i)
            entries = {k: spread(columns[k][own], i) for k in range(j + 1, stop)}
            for g in range(own, tiles):
                ratio = columns[j][g] * reciprocal
                if g == own:
                    ratio = jnp.where(sublane > i, ratio, 0.0)
                work[g] = work[g] - ratio * row
                for k in range(j + 1, stop):
                    columns[k][g] = columns[k][g] - ratio * entries[k]
    for g in range(tiles):
        scaled = work[g] * lax.rsqrt(diagonal[g])
        inverse_ref[SUBLANES * g : SUBLANES * (g + 1), :] = scaled[:, count : 2 * count]


def basis_kernel(inverse_ref, gram_ref, basis_ref, image_ref, basis_new_ref, image_start_ref, start_ref):
    inverse = inverse_ref[...]
    count, old = inverse.shape[0], image_ref.shape[0]
    basis_new_ref[...] = multiply(inverse, basis_ref[...])
    image_start_ref[...] = multiply(inverse[:, :old], image_ref[...])
    coupling = gram_ref[:, count : count + old]
    start_ref[...] = contract_last(multiply(inverse, coupling), inverse[:, :old])


def image_kernel(scale, basis_new_ref, *refs):
    *sums_refs, image_ref, part_ref = refs
    blocks = sums_refs[0].shape[0]
    summed = pairwise([ref[:blocks] for ref in sums_refs])
    image = jnp.concatenate([summed[b] for b in range(summed.shape[0])], axis=1)
    image_ref[...] = image
    vecs, count = image.shape[0], basis_new_ref.shape[0]
    part = contract_last(image, basis_new_ref[...]) * scale
    part = jnp.concatenate([part, jnp.zeros((vecs, LANES - count), jnp.float32)], axis=1)
    part_ref[...] = jnp.broadcast_to(part[None], part_ref.shape)


def finish_kernel(
    inverse_ref, basis_new_ref, image_start_ref, image_ref, start_ref, parts_ref,
    projected_hbm, basis_new_hbm, image_new_hbm, projected_vmem, image_new_vmem, sems,
):
    basis_copy = pltpu.make_async_copy(basis_new_ref, basis_new_hbm, sems.at[0])
    basis_copy.start()
    vecs = image_ref.shape[0]
    count = inverse_ref.shape[0]
    last = inverse_ref[...][:, count - vecs :]
    image_new = image_start_ref[...]
    for k in range(vecs):
        image_new = image_new + last[:, k : k + 1] * image_ref[k : k + 1, :]
    image_new_vmem[...] = image_new
    image_copy = pltpu.make_async_copy(image_new_vmem, image_new_hbm, sems.at[1])
    image_copy.start()
    total = jnp.sum(parts_ref[...], axis=0)
    new = lax.dot_general(
        total[:, :count],
        last,
        (((0,), (1,)), ((), ())),
        precision=HIGHEST,
        preferred_element_type=jnp.float32,
    )
    projected_vmem[...] = start_ref[...] + new
    projected_copy = pltpu.make_async_copy(projected_vmem, projected_hbm, sems.at[2])
    projected_copy.start()
    basis_copy.wait()
    image_copy.wait()
    projected_copy.wait()


def call(kernel, outs, *args, after=(), time=0.0, smem=0, from_hbm=False, to_hbm=False, scratch=()):
    operand = pl.BlockSpec(memory_space=pltpu.HBM if from_hbm else pltpu.VMEM)
    result = pl.BlockSpec(memory_space=pltpu.HBM if to_hbm else pltpu.VMEM)
    scalars = pl.BlockSpec(memory_space=pltpu.SMEM)
    if from_hbm:
        args = [pltpu.with_memory_space_constraint(arg, pltpu.HBM) for arg in args]
    result_specs = [scalars if hasattr(o, "dtype") else result for o in outs]
    outs = [o if hasattr(o, "dtype") else jax.ShapeDtypeStruct(o, jnp.float32) for o in outs]
    n_after = len(after)

    def body(*refs):
        kernel(*refs[n_after:])

    return pl.pallas_call(
        body,
        out_shape=outs,
        in_specs=[operand] * n_after + [scalars] * smem + [operand] * (len(args) - smem),
        out_specs=result_specs,
        scratch_shapes=scratch,
        compiler_params=pltpu.CompilerParams(vmem_limit_bytes=VMEM_LIMIT),
        cost_estimate=pl.CostEstimate(
            flops=int(time * FLOPS_PER_US), bytes_accessed=int(time * BYTES_PER_US), transcendentals=0
        ),
        name=(kernel.func if hasattr(kernel, "func") else kernel).__name__[:-7],
    )(*after, *args)


def bits_of(size):
    return [1 << j for j in range(size.bit_length() - 1)]


def swap(array, axis, mask):
    size = lax.axis_size(axis)
    return lax.ppermute(array, axis, [(i, i ^ mask) for i in range(size)])


def local(tile_blocks, tile_rows, tile_cols, trial_vectors, basis_old, image_old):
    tile_size = tile_blocks.shape[1]
    vecs, width = trial_vectors.shape
    old = basis_old.shape[0]
    count = old + vecs
    blocks = width // tile_size
    n_row, n_col = lax.axis_size("row"), lax.axis_size("col")
    scale = 1.0 / float(width * n_row * n_col)
    row_bits, col_bits = [m | 1 for m in bits_of(n_row)], bits_of(n_col)
    gather_row = row_bits[1:] + row_bits[:1]
    scatter_row, scatter_col = row_bits, col_bits
    grams = count // vecs
    tile = (vecs, tile_size)

    places = pltpu.SMEM(tile_rows.shape, tile_rows.dtype)
    wide, basis_all, image_kept, rows_kept, cols_kept = call(
        load_kernel,
        [(blocks, *tile), (count, width), (old, width), places, places],
        trial_vectors,
        basis_old,
        image_old,
        tile_rows,
        tile_cols,
        time=1.0,
        from_hbm=True,
        scratch=[
            pltpu.VMEM((vecs, width), trial_vectors.dtype),
            pltpu.VMEM((old, width), jnp.float32),
            pltpu.SemaphoreType.DMA((5,)),
        ],
    )
    (own,) = call(
        functools.partial(gram_kernel, scale),
        [(blocks + grams, *tile)],
        wide,
        basis_all,
        image_kept,
        time=0.5,
    )
    row_got = [swap(own, "col", m) for m in range(1, n_col)]
    col_got = [wide]
    for m in gather_row:
        col_got.append(swap(jnp.concatenate(col_got, axis=0), "row", m))

    half_row, half_col = blocks * n_row // 2, blocks * n_col // 2
    col_kept, col_sent = call(
        functools.partial(
            backward_kernel, col_bits, scatter_row[::-1], n_row, blocks, len(row_got)
        ),
        [(half_row, *tile), (half_row + grams, *tile)],
        rows_kept,
        cols_kept,
        tile_blocks,
        own,
        *row_got,
        time=1.0,
        smem=2,
        scratch=[
            pltpu.VMEM((2 * half_col, *tile), jnp.float32),
            pltpu.VMEM((2 * half_row, *tile), jnp.float32),
        ],
    )
    row_kept, row_sent = call(
        functools.partial(
            forward_kernel, scatter_col[::-1], gather_row, n_row, blocks, len(col_got)
        ),
        [(half_col, *tile)] * 2,
        rows_kept,
        cols_kept,
        tile_blocks,
        *col_got,
        time=1.0,
        smem=2,
        scratch=[
            pltpu.VMEM((2 * half_row, *tile), jnp.float32),
            pltpu.VMEM((2 * half_col, *tile), jnp.float32),
        ],
    )
    forward_done = row_kept
    for i, m in enumerate(scatter_row[:-1]):
        half_row //= 2
        col_kept, col_sent = call(
            fold_kernel,
            [(half_row, *tile), (half_row + grams, *tile)],
            col_kept,
            col_sent,
            swap(col_sent, "row", m),
            after=[forward_done] if i == n_row.bit_length() - 3 else [],
            time=0.1,
        )
    col_parts = [col_kept, swap(col_sent, "row", scatter_row[-1])]
    for m in scatter_col[:-1]:
        half_col //= 2
        row_kept, row_sent = call(
            fold_kernel,
            [(half_col, *tile)] * 2,
            row_kept,
            row_sent,
            swap(row_sent, "col", m),
            time=0.1,
        )
    row_parts = [row_kept, swap(row_sent, "col", scatter_col[-1])]

    inverse, gram = call(
        functools.partial(factor_kernel, count, blocks),
        [(count, count), (count, LANES)],
        col_sent,
        col_parts[1],
        time=1.1,
    )
    basis_new, image_start, start = call(
        basis_kernel,
        [(count, width), (count, width), (count, count)],
        inverse,
        gram,
        basis_all,
        image_kept,
    )
    image, part = call(
        functools.partial(image_kernel, scale),
        [(vecs, width), (n_row * n_col, vecs, LANES)],
        basis_new,
        *row_parts,
        *col_parts,
    )
    parts = lax.all_to_all(part, ("row", "col"), split_axis=0, concat_axis=0, tiled=True)
    return call(
        finish_kernel,
        [(count, count), (count, width), (count, width)],
        inverse,
        basis_new,
        image_start,
        image,
        start,
        parts,
        to_hbm=True,
        scratch=[
            pltpu.VMEM((count, count), jnp.float32),
            pltpu.VMEM((count, width), jnp.float32),
            pltpu.SemaphoreType.DMA((3,)),
        ],
    )


def solution(mesh):
    in_specs = (
        P(("row", "col"), None, None),
        P(("row", "col")),
        P(("row", "col")),
        P(None, ("col", "row")),
        P(None, ("col", "row")),
        P(None, ("col", "row")),
    )
    out_specs = (P(), P(None, ("col", "row")), P(None, ("col", "row")))
    return jax.shard_map(local, mesh=mesh, in_specs=in_specs, out_specs=out_specs, check_vma=False)
```

```python
import functools

import jax
import jax.numpy as jnp
from jax import lax
from jax.experimental import pallas as pl
from jax.experimental.pallas import tpu as pltpu
from jax.sharding import PartitionSpec as P

HIGHEST = lax.Precision.HIGHEST
LANES = 128
SUBLANES = 8
PANEL = 16
GROUP = 2
FLOPS_PER_US = 1.1e9
BYTES_PER_US = 3.6e6
VMEM_LIMIT = 32 * 1024 * 1024


def three_parts(wide):
    high = wide.astype(jnp.bfloat16)
    rest = wide - high.astype(jnp.float32)
    middle = rest.astype(jnp.bfloat16)
    return high, middle, (rest - middle.astype(jnp.float32)).astype(jnp.bfloat16)


def product(left, right, contract):
    rows = left.shape[0]
    padding = -rows % 16
    if padding:
        left = jnp.concatenate([left, jnp.zeros((padding, left.shape[1]), left.dtype)], axis=0)
    size = rows + padding
    high, middle, low = three_parts(left)
    stacked = jnp.concatenate([high, middle, low], axis=0)
    sums = [
        lax.dot_general(
            stacked[: size * (3 - i)],
            part,
            (((1,), (contract,)), ((), ())),
            preferred_element_type=jnp.float32,
        )
        for i, part in enumerate(three_parts(right))
    ]
    small = (sums[0][2 * size : 2 * size + rows] + sums[1][size : size + rows]) + sums[2][:rows]
    middle = sums[0][size : size + rows] + sums[1][:rows]
    return sums[0][:rows] + (middle + small)


def contract_last(left, right):
    return product(left, right, 1)


def multiply(left, right):
    return product(left, right, 0)


def pairwise(terms):
    while len(terms) > 1:
        terms = [sum(terms[i + 1 : i + 2], terms[i]) for i in range(0, len(terms), 2)]
    return terms[0]


def side_by_side(blocks_ref):
    return jnp.concatenate([blocks_ref[b] for b in range(blocks_ref.shape[0])], axis=1)


def load_kernel(
    trial_hbm, basis_hbm, image_hbm, rows_hbm, cols_hbm,
    wide_ref, narrow_ref, basis_ref, image_ref, rows_ref, cols_ref, trial_vmem, basis_vmem, sems,
):
    copies = [
        pltpu.make_async_copy(source, target, sems.at[i])
        for i, (source, target) in enumerate(
            [
                (trial_hbm, trial_vmem),
                (basis_hbm, basis_vmem),
                (image_hbm, image_ref),
                (rows_hbm, rows_ref),
                (cols_hbm, cols_ref),
            ]
        )
    ]
    for copy in copies:
        copy.start()
    copies[0].wait()
    trial = trial_vmem[...].astype(jnp.float32)
    for b in range(wide_ref.shape[0]):
        wide_ref[b] = trial[:, b * LANES : (b + 1) * LANES]
    by_blocks = [trial[:, b * LANES : (b + 1) * LANES] for b in range(wide_ref.shape[0])]
    narrow_ref[...] = jnp.concatenate(by_blocks, axis=0).astype(narrow_ref.dtype)
    copies[1].wait()
    basis_ref[...] = jnp.concatenate([basis_vmem[...], trial], axis=0)
    for copy in copies[2:]:
        copy.wait()


def gram_kernel(scale, wide_ref, narrow_ref, basis_ref, image_ref, sent_ref, again_ref):
    blocks, vecs = wide_ref.shape[:2]
    basis_all = basis_ref[...]
    images = image_ref[...]
    count = basis_all.shape[0]
    used = count + images.shape[0]
    filler = jnp.zeros((LANES - used, images.shape[1]), jnp.float32)
    gram = contract_last(basis_all, jnp.concatenate([basis_all, images, filler], axis=0)) * scale
    third, top = count // 3, count - count // 3
    middle = (top + used) // 2
    folded = jnp.concatenate([gram[top:, top:middle], gram[top:, middle:used]], axis=0)
    unused = jnp.zeros((top, LANES - used - (middle - top)), jnp.float32)
    packed = jnp.concatenate([gram[:top, :used], folded, unused], axis=1)
    again_ref[...] = narrow_ref[...]
    sent_ref[:blocks] = wide_ref[...]
    for i in range(top // vecs):
        sent_ref[blocks + i] = packed[i * vecs : (i + 1) * vecs]


def unpack(packed, count, old):
    third, top = count // 3, count - count // 3
    used = count + old
    middle = (top + used) // 2
    width = middle - top
    parts = [
        packed[:, top:count].T,
        packed[:third, used : used + width],
        packed[third:, used : used + width],
        jnp.zeros((third, LANES - used), jnp.float32),
    ]
    return jnp.concatenate([packed, jnp.concatenate(parts, axis=1)], axis=0)


def split(index, size):
    return index >> (size.bit_length() - 1), index & (size - 1)


def place(apart, masks):
    crossed = any(m & (m - 1) for m in masks)
    at = 0
    for j, m in enumerate(masks):
        bit = apart >> (m.bit_length() - 1)
        if m == 1 and crossed:
            for k in range(1, len(masks)):
                bit = bit ^ (apart >> k)
        at = at + ((bit & 1) << j)
    return at


def tiles_product(contract, by_rows, by_cols, n_row, blocks, scalars, tiles_ref, vecs_ref, sums_ref):
    rows_ref, cols_ref = scalars
    sums_ref[...] = jnp.zeros_like(sums_ref)
    row, col = lax.axis_index("row"), lax.axis_index("col")
    places = []
    for t in range(tiles_ref.shape[0]):
        row_piece, row_inner = split(rows_ref[t], blocks)
        col_piece, col_inner = split(cols_ref[t] - col * (blocks * n_row), blocks)
        at_row = place(split(row_piece, n_row)[0] ^ col, by_rows) * blocks + row_inner
        at_col = place(col_piece ^ row, by_cols) * blocks + col_inner
        places.append((at_col, at_row) if contract else (at_row, at_col))
    vecs, size = vecs_ref.shape[1:]
    for t in range(0, len(places), GROUP):
        group = range(t, min(t + GROUP, len(places)))
        picked = jnp.concatenate([vecs_ref[places[u][0]] for u in group], axis=0)
        products = lax.dot_general(
            picked.astype(jnp.bfloat16),
            jnp.concatenate([tiles_ref[u] for u in group], axis=1 - contract),
            (((1,), (contract,)), ((), ())),
            preferred_element_type=jnp.float32,
        )
        for i, u in enumerate(group):
            target = places[u][1]
            own = products[i * vecs : (i + 1) * vecs, i * size : (i + 1) * size]
            sums_ref[target] = sums_ref[target] + own


def backward_kernel(by_rows, by_cols, n_row, blocks, n_got, *refs):
    scalars, tiles_ref, own_ref = refs[:2], refs[2], refs[3]
    got_refs = refs[4 : 4 + n_got]
    kept_ref, sent_ref, vecs_ref, sums_ref = refs[4 + n_got :]
    for p, ref in enumerate([own_ref, *got_refs]):
        vecs_ref[p * blocks : (p + 1) * blocks] = ref[:blocks]
    tiles_product(0, by_rows, by_cols, n_row, blocks, scalars, tiles_ref, vecs_ref, sums_ref)
    half = kept_ref.shape[0]
    kept_ref[...] = sums_ref[:half]
    sent_ref[:half] = sums_ref[half:]
    sent_ref[half:] = pairwise([ref[blocks:] for ref in (own_ref, *got_refs)])


def forward_kernel(by_rows, by_cols, n_row, blocks, n_got, *refs):
    scalars, tiles_ref = refs[:2], refs[2]
    got_refs = refs[3 : 3 + n_got]
    *piece_refs, vecs_ref, sums_ref = refs[3 + n_got :]
    at = 0
    vecs = vecs_ref.shape[1]
    for ref in got_refs:
        got = ref[...].astype(jnp.float32)
        for b in range(got.shape[0] // vecs):
            vecs_ref[at + b] = got[b * vecs : (b + 1) * vecs]
        at += got.shape[0] // vecs
    tiles_product(1, by_rows, by_cols, n_row, blocks, scalars, tiles_ref, vecs_ref, sums_ref)
    at = 0
    for ref in piece_refs:
        ref[...] = sums_ref[at : at + ref.shape[0]]
        at += ref.shape[0]


def fold_kernel(kept_ref, sent_ref, got_ref, kept_next_ref, sent_next_ref):
    size, half = kept_ref.shape[0], kept_next_ref.shape[0]
    kept_next_ref[...] = kept_ref[:half] + got_ref[:half]
    sent_next_ref[:half] = kept_ref[half:] + got_ref[half:size]
    if sent_next_ref.shape[0] > half:
        sent_next_ref[half:] = sent_ref[size:] + got_ref[size:]


def factor_kernel(count, old, blocks, sent_ref, got_ref, inverse_ref, gram_ref):
    summed = sent_ref[blocks:] + got_ref[blocks:]
    packed = jnp.concatenate([summed[i] for i in range(summed.shape[0])], axis=0)
    gram = unpack(packed, count, old)
    gram_ref[...] = gram
    row_id = lax.broadcasted_iota(jnp.int32, (count, LANES), 0)
    lane_id = lax.broadcasted_iota(jnp.int32, (count, LANES), 1)
    identity = jnp.where(lane_id == row_id + count, 1.0, 0.0)
    work = jnp.where(lane_id < count, gram, identity)
    tiles = count // SUBLANES
    work = [work[SUBLANES * g : SUBLANES * (g + 1)] for g in range(tiles)]
    sublane = lax.broadcasted_iota(jnp.int32, (SUBLANES, LANES), 0)
    diagonal = [jnp.ones((SUBLANES, LANES), jnp.float32)] * tiles

    def spread(tile, i):
        return jnp.broadcast_to(tile[i : i + 1, :], (SUBLANES, LANES))

    for start in range(0, count, PANEL):
        stop = min(start + PANEL, count)
        first = start // SUBLANES
        columns = {
            j: {
                g: jnp.broadcast_to(work[g][:, j : j + 1], (SUBLANES, LANES))
                for g in range(first, tiles)
            }
            for j in range(start, stop)
        }
        for j in range(start, stop):
            i, own = j % SUBLANES, j // SUBLANES
            pivot = spread(columns[j][own], i)
            diagonal[own] = jnp.where(sublane == i, pivot, diagonal[own])
            reciprocal = 1.0 / pivot
            row = spread(work[own], i)
            entries = {k: spread(columns[k][own], i) for k in range(j + 1, stop)}
            for g in range(own, tiles):
                ratio = columns[j][g] * reciprocal
                if g == own:
                    ratio = jnp.where(sublane > i, ratio, 0.0)
                work[g] = work[g] - ratio * row
                for k in range(j + 1, stop):
                    columns[k][g] = columns[k][g] - ratio * entries[k]
    for g in range(tiles):
        scaled = work[g] * lax.rsqrt(diagonal[g])
        inverse_ref[SUBLANES * g : SUBLANES * (g + 1), :] = scaled[:, count : 2 * count]


def basis_kernel(inverse_ref, gram_ref, basis_ref, image_ref, basis_new_ref, image_start_ref, start_ref):
    inverse = inverse_ref[...]
    count, old = inverse.shape[0], image_ref.shape[0]
    basis_new_ref[...] = multiply(inverse, basis_ref[...])
    image_start_ref[...] = multiply(inverse[:, :old], image_ref[...])
    coupling = gram_ref[:, count : count + old]
    start_ref[...] = contract_last(multiply(inverse, coupling), inverse[:, :old])


def image_kernel(scale, basis_new_ref, *refs):
    *sums_refs, image_ref, part_ref = refs
    blocks = sums_refs[0].shape[0]
    summed = pairwise([ref[:blocks] for ref in sums_refs])
    image = jnp.concatenate([summed[b] for b in range(summed.shape[0])], axis=1)
    image_ref[...] = image
    vecs, count = image.shape[0], basis_new_ref.shape[0]
    part = contract_last(image, basis_new_ref[...]) * scale
    part = jnp.concatenate([part, jnp.zeros((vecs, LANES // 2 - count), jnp.float32)], axis=1)
    part = jnp.concatenate([part[: vecs // 2], part[vecs // 2 :]], axis=1)
    part_ref[...] = jnp.broadcast_to(part[None], part_ref.shape)


def finish_kernel(
    inverse_ref, basis_new_ref, image_start_ref, image_ref, start_ref, parts_ref,
    projected_hbm, basis_new_hbm, image_new_hbm, projected_vmem, image_new_vmem, sems,
):
    basis_copy = pltpu.make_async_copy(basis_new_ref, basis_new_hbm, sems.at[0])
    basis_copy.start()
    vecs = image_ref.shape[0]
    count = inverse_ref.shape[0]
    last = inverse_ref[...][:, count - vecs :]
    image_new = image_start_ref[...]
    for k in range(vecs):
        image_new = image_new + last[:, k : k + 1] * image_ref[k : k + 1, :]
    image_new_vmem[...] = image_new
    image_copy = pltpu.make_async_copy(image_new_vmem, image_new_hbm, sems.at[1])
    image_copy.start()
    total = jnp.sum(parts_ref[...], axis=0)
    total = jnp.concatenate([total[:, : LANES // 2], total[:, LANES // 2 :]], axis=0)
    new = lax.dot_general(
        total[:, :count],
        last,
        (((0,), (1,)), ((), ())),
        precision=HIGHEST,
        preferred_element_type=jnp.float32,
    )
    projected_vmem[...] = start_ref[...] + new
    projected_copy = pltpu.make_async_copy(projected_vmem, projected_hbm, sems.at[2])
    projected_copy.start()
    basis_copy.wait()
    image_copy.wait()
    projected_copy.wait()


def call(kernel, outs, *args, after=(), time=0.0, smem=0, from_hbm=False, to_hbm=False, scratch=()):
    operand = pl.BlockSpec(memory_space=pltpu.HBM if from_hbm else pltpu.VMEM)
    result = pl.BlockSpec(memory_space=pltpu.HBM if to_hbm else pltpu.VMEM)
    scalars = pl.BlockSpec(memory_space=pltpu.SMEM)
    if from_hbm:
        args = [pltpu.with_memory_space_constraint(arg, pltpu.HBM) for arg in args]
    result_specs = [scalars if getattr(o, "dtype", None) == jnp.int32 else result for o in outs]
    outs = [o if hasattr(o, "dtype") else jax.ShapeDtypeStruct(o, jnp.float32) for o in outs]
    n_after = len(after)

    def body(*refs):
        kernel(*refs[n_after:])

    return pl.pallas_call(
        body,
        out_shape=outs,
        in_specs=[operand] * n_after + [scalars] * smem + [operand] * (len(args) - smem),
        out_specs=result_specs,
        scratch_shapes=scratch,
        compiler_params=pltpu.CompilerParams(vmem_limit_bytes=VMEM_LIMIT),
        cost_estimate=pl.CostEstimate(
            flops=int(time * FLOPS_PER_US), bytes_accessed=int(time * BYTES_PER_US), transcendentals=0
        ),
        name=(kernel.func if hasattr(kernel, "func") else kernel).__name__[:-7],
    )(*after, *args)


def bits_of(size):
    return [1 << j for j in range(size.bit_length() - 1)]


def swap(array, axis, mask):
    size = lax.axis_size(axis)
    return lax.ppermute(array, axis, [(i, i ^ mask) for i in range(size)])


def local(tile_blocks, tile_rows, tile_cols, trial_vectors, basis_old, image_old):
    tile_size = tile_blocks.shape[1]
    vecs, width = trial_vectors.shape
    old = basis_old.shape[0]
    count = old + vecs
    blocks = width // tile_size
    n_row, n_col = lax.axis_size("row"), lax.axis_size("col")
    scale = 1.0 / float(width * n_row * n_col)
    row_bits, col_bits = [m | 1 for m in bits_of(n_row)], bits_of(n_col)
    gather_row = row_bits[1:] + row_bits[:1]
    scatter_row, scatter_col = row_bits, col_bits
    grams = (count - count // 3) // vecs
    tile = (vecs, tile_size)

    narrow_shape = jax.ShapeDtypeStruct((blocks * vecs, tile_size), trial_vectors.dtype)
    places = pltpu.SMEM(tile_rows.shape, tile_rows.dtype)
    wide, narrow, basis_all, image_kept, rows_kept, cols_kept = call(
        load_kernel,
        [(blocks, *tile), narrow_shape, (count, width), (old, width), places, places],
        trial_vectors,
        basis_old,
        image_old,
        tile_rows,
        tile_cols,
        time=1.0,
        from_hbm=True,
        scratch=[
            pltpu.VMEM((vecs, width), trial_vectors.dtype),
            pltpu.VMEM((old, width), jnp.float32),
            pltpu.SemaphoreType.DMA((5,)),
        ],
    )
    own, again = call(
        functools.partial(gram_kernel, scale),
        [(blocks + grams, *tile), narrow_shape],
        wide,
        narrow,
        basis_all,
        image_kept,
        time=0.5,
    )
    row_got = [swap(own, "col", m) for m in range(1, n_col)]
    col_got = [again]
    for m in gather_row:
        col_got.append(swap(jnp.concatenate(col_got, axis=0), "row", m))

    half_row, half_col = blocks * n_row // 2, blocks * n_col // 2
    col_kept, col_sent = call(
        functools.partial(
            backward_kernel, col_bits, scatter_row[::-1], n_row, blocks, len(row_got)
        ),
        [(half_row, *tile), (half_row + grams, *tile)],
        rows_kept,
        cols_kept,
        tile_blocks,
        own,
        *row_got,
        time=1.0,
        smem=2,
        scratch=[
            pltpu.VMEM((2 * half_col, *tile), jnp.float32),
            pltpu.VMEM((2 * half_row, *tile), jnp.float32),
        ],
    )
    row_kept, row_sent = call(
        functools.partial(
            forward_kernel, scatter_col[::-1], gather_row, n_row, blocks, len(col_got)
        ),
        [(half_col, *tile)] * 2,
        rows_kept,
        cols_kept,
        tile_blocks,
        *col_got,
        time=1.0,
        smem=2,
        scratch=[
            pltpu.VMEM((2 * half_row, *tile), jnp.float32),
            pltpu.VMEM((2 * half_col, *tile), jnp.float32),
        ],
    )
    forward_done = row_kept
    for i, m in enumerate(scatter_row[:-1]):
        half_row //= 2
        col_kept, col_sent = call(
            fold_kernel,
            [(half_row, *tile), (half_row + grams, *tile)],
            col_kept,
            col_sent,
            swap(col_sent, "row", m),
            after=[forward_done] if i == n_row.bit_length() - 3 else [],
            time=0.1,
        )
    col_parts = [col_kept, swap(col_sent, "row", scatter_row[-1])]
    for m in scatter_col[:-1]:
        half_col //= 2
        row_kept, row_sent = call(
            fold_kernel,
            [(half_col, *tile)] * 2,
            row_kept,
            row_sent,
            swap(row_sent, "col", m),
            time=0.1,
        )
    row_parts = [row_kept, swap(row_sent, "col", scatter_col[-1])]

    inverse, gram = call(
        functools.partial(factor_kernel, count, old, blocks),
        [(count, count), (count, LANES)],
        col_sent,
        col_parts[1],
        time=1.1,
    )
    basis_new, image_start, start = call(
        basis_kernel,
        [(count, width), (count, width), (count, count)],
        inverse,
        gram,
        basis_all,
        image_kept,
    )
    image, part = call(
        functools.partial(image_kernel, scale),
        [(vecs, width), (n_row * n_col, vecs // 2, LANES)],
        basis_new,
        *row_parts,
        *col_parts,
    )
    parts = lax.all_to_all(part, ("row", "col"), split_axis=0, concat_axis=0, tiled=True)
    return call(
        finish_kernel,
        [(count, count), (count, width), (count, width)],
        inverse,
        basis_new,
        image_start,
        image,
        start,
        parts,
        to_hbm=True,
        scratch=[
            pltpu.VMEM((count, count), jnp.float32),
            pltpu.VMEM((count, width), jnp.float32),
            pltpu.SemaphoreType.DMA((3,)),
        ],
    )


def solution(mesh):
    in_specs = (
        P(("row", "col"), None, None),
        P(("row", "col")),
        P(("row", "col")),
        P(None, ("col", "row")),
        P(None, ("col", "row")),
        P(None, ("col", "row")),
    )
    out_specs = (P(), P(None, ("col", "row")), P(None, ("col", "row")))
    return jax.shard_map(local, mesh=mesh, in_specs=in_specs, out_specs=out_specs, check_vma=False)
```

```python
import functools

import jax
import jax.numpy as jnp
from jax import lax
from jax.experimental import pallas as pl
from jax.experimental.pallas import tpu as pltpu
from jax.sharding import PartitionSpec as P

HIGHEST = lax.Precision.HIGHEST
LANES = 128
SUBLANES = 8
PANEL = 16
GROUP = 2
FLOPS_PER_US = 1.1e9
BYTES_PER_US = 3.6e6
VMEM_LIMIT = 32 * 1024 * 1024


def three_parts(wide):
    high = wide.astype(jnp.bfloat16)
    rest = wide - high.astype(jnp.float32)
    middle = rest.astype(jnp.bfloat16)
    return high, middle, (rest - middle.astype(jnp.float32)).astype(jnp.bfloat16)


def product(left, right, contract):
    rows = left.shape[0]
    padding = -rows % 16
    if padding:
        left = jnp.concatenate([left, jnp.zeros((padding, left.shape[1]), left.dtype)], axis=0)
    size = rows + padding
    high, middle, low = three_parts(left)
    stacked = jnp.concatenate([high, middle, low], axis=0)
    sums = [
        lax.dot_general(
            stacked[: size * (3 - i)],
            part,
            (((1,), (contract,)), ((), ())),
            preferred_element_type=jnp.float32,
        )
        for i, part in enumerate(three_parts(right))
    ]
    small = (sums[0][2 * size : 2 * size + rows] + sums[1][size : size + rows]) + sums[2][:rows]
    middle = sums[0][size : size + rows] + sums[1][:rows]
    return sums[0][:rows] + (middle + small)


def contract_last(left, right):
    return product(left, right, 1)


def multiply(left, right):
    return product(left, right, 0)


def pairwise(terms):
    while len(terms) > 1:
        terms = [sum(terms[i + 1 : i + 2], terms[i]) for i in range(0, len(terms), 2)]
    return terms[0]


def side_by_side(blocks_ref):
    return jnp.concatenate([blocks_ref[b] for b in range(blocks_ref.shape[0])], axis=1)


def load_kernel(
    trial_hbm, basis_hbm, image_hbm, rows_hbm, cols_hbm,
    wide_ref, narrow_ref, basis_ref, image_ref, rows_ref, cols_ref, trial_vmem, basis_vmem, sems,
):
    copies = [
        pltpu.make_async_copy(source, target, sems.at[i])
        for i, (source, target) in enumerate(
            [
                (trial_hbm, trial_vmem),
                (basis_hbm, basis_vmem),
                (image_hbm, image_ref),
                (rows_hbm, rows_ref),
                (cols_hbm, cols_ref),
            ]
        )
    ]
    for copy in copies:
        copy.start()
    copies[0].wait()
    trial = trial_vmem[...].astype(jnp.float32)
    for b in range(wide_ref.shape[0]):
        wide_ref[b] = trial[:, b * LANES : (b + 1) * LANES]
    by_blocks = [trial[:, b * LANES : (b + 1) * LANES] for b in range(wide_ref.shape[0])]
    narrow_ref[...] = jnp.concatenate(by_blocks, axis=0).astype(narrow_ref.dtype)
    copies[1].wait()
    basis_ref[...] = jnp.concatenate([basis_vmem[...], trial], axis=0)
    for copy in copies[2:]:
        copy.wait()


def gram_kernel(scale, wide_ref, narrow_ref, basis_ref, image_ref, sent_ref, again_ref):
    blocks, vecs = wide_ref.shape[:2]
    basis_all = basis_ref[...]
    images = image_ref[...]
    count = basis_all.shape[0]
    used = count + images.shape[0]
    filler = jnp.zeros((LANES - used, images.shape[1]), jnp.float32)
    gram = contract_last(basis_all, jnp.concatenate([basis_all, images, filler], axis=0)) * scale
    third, top = count // 3, count - count // 3
    middle = (top + used) // 2
    folded = jnp.concatenate([gram[top:, top:middle], gram[top:, middle:used]], axis=0)
    unused = jnp.zeros((top, LANES - used - (middle - top)), jnp.float32)
    packed = jnp.concatenate([gram[:top, :used], folded, unused], axis=1)
    again_ref[...] = narrow_ref[...]
    sent_ref[:blocks] = wide_ref[...]
    for i in range(top // vecs):
        sent_ref[blocks + i] = packed[i * vecs : (i + 1) * vecs]


def unpack(packed, count, old):
    third, top = count // 3, count - count // 3
    used = count + old
    middle = (top + used) // 2
    width = middle - top
    parts = [
        packed[:, top:count].T,
        packed[:third, used : used + width],
        packed[third:, used : used + width],
        jnp.zeros((third, LANES - used), jnp.float32),
    ]
    return jnp.concatenate([packed, jnp.concatenate(parts, axis=1)], axis=0)


def split(index, size):
    return index >> (size.bit_length() - 1), index & (size - 1)


def place(apart, masks):
    crossed = any(m & (m - 1) for m in masks)
    at = 0
    for j, m in enumerate(masks):
        bit = apart >> (m.bit_length() - 1)
        if m == 1 and crossed:
            for k in range(1, len(masks)):
                bit = bit ^ (apart >> k)
        at = at + ((bit & 1) << j)
    return at


def tiles_product(contract, by_rows, by_cols, n_row, blocks, scalars, tiles_ref, vecs_ref, sums_ref):
    rows_ref, cols_ref = scalars
    sums_ref[...] = jnp.zeros_like(sums_ref)
    row, col = lax.axis_index("row"), lax.axis_index("col")
    places = []
    for t in range(tiles_ref.shape[0]):
        row_piece, row_inner = split(rows_ref[t], blocks)
        col_piece, col_inner = split(cols_ref[t] - col * (blocks * n_row), blocks)
        at_row = place(split(row_piece, n_row)[0] ^ col, by_rows) * blocks + row_inner
        at_col = place(col_piece ^ row, by_cols) * blocks + col_inner
        places.append((at_col, at_row) if contract else (at_row, at_col))
    vecs, size = vecs_ref.shape[1:]
    for t in range(0, len(places), GROUP):
        group = range(t, min(t + GROUP, len(places)))
        picked = jnp.concatenate([vecs_ref[places[u][0]] for u in group], axis=0)
        products = lax.dot_general(
            picked.astype(jnp.bfloat16),
            jnp.concatenate([tiles_ref[u] for u in group], axis=1 - contract),
            (((1,), (contract,)), ((), ())),
            preferred_element_type=jnp.float32,
        )
        for i, u in enumerate(group):
            target = places[u][1]
            own = products[i * vecs : (i + 1) * vecs, i * size : (i + 1) * size]
            sums_ref[target] = sums_ref[target] + own


def backward_kernel(by_rows, by_cols, n_row, blocks, n_got, *refs):
    scalars, tiles_ref, own_ref = refs[:2], refs[2], refs[3]
    got_refs = refs[4 : 4 + n_got]
    kept_ref, sent_ref, vecs_ref, sums_ref = refs[4 + n_got :]
    for p, ref in enumerate([own_ref, *got_refs]):
        vecs_ref[p * blocks : (p + 1) * blocks] = ref[:blocks]
    tiles_product(0, by_rows, by_cols, n_row, blocks, scalars, tiles_ref, vecs_ref, sums_ref)
    half = kept_ref.shape[0]
    kept_ref[...] = sums_ref[:half]
    sent_ref[:half] = sums_ref[half:]
    sent_ref[half:] = pairwise([ref[blocks:] for ref in (own_ref, *got_refs)])


def forward_kernel(by_rows, by_cols, n_row, blocks, n_got, *refs):
    scalars, tiles_ref = refs[:2], refs[2]
    got_refs = refs[3 : 3 + n_got]
    *piece_refs, vecs_ref, sums_ref = refs[3 + n_got :]
    at = 0
    vecs = vecs_ref.shape[1]
    for ref in got_refs:
        got = ref[...].astype(jnp.float32)
        for b in range(got.shape[0] // vecs):
            vecs_ref[at + b] = got[b * vecs : (b + 1) * vecs]
        at += got.shape[0] // vecs
    tiles_product(1, by_rows, by_cols, n_row, blocks, scalars, tiles_ref, vecs_ref, sums_ref)
    at = 0
    for ref in piece_refs:
        ref[...] = sums_ref[at : at + ref.shape[0]]
        at += ref.shape[0]


def fold_kernel(kept_ref, sent_ref, got_ref, kept_next_ref, sent_next_ref):
    size, half = kept_ref.shape[0], kept_next_ref.shape[0]
    kept_next_ref[...] = kept_ref[:half] + got_ref[:half]
    sent_next_ref[:half] = kept_ref[half:] + got_ref[half:size]
    if sent_next_ref.shape[0] > half:
        sent_next_ref[half:] = sent_ref[size:] + got_ref[size:]


def factor_kernel(count, old, blocks, sent_ref, got_ref, inverse_ref, gram_ref):
    summed = sent_ref[blocks:] + got_ref[blocks:]
    packed = jnp.concatenate([summed[i] for i in range(summed.shape[0])], axis=0)
    gram = unpack(packed, count, old)
    gram_ref[...] = gram
    row_id = lax.broadcasted_iota(jnp.int32, (count, LANES), 0)
    lane_id = lax.broadcasted_iota(jnp.int32, (count, LANES), 1)
    identity = jnp.where(lane_id == row_id + count, 1.0, 0.0)
    work = jnp.where(lane_id < count, gram, identity)
    tiles = count // SUBLANES
    work = [work[SUBLANES * g : SUBLANES * (g + 1)] for g in range(tiles)]
    sublane = lax.broadcasted_iota(jnp.int32, (SUBLANES, LANES), 0)
    diagonal = [jnp.ones((SUBLANES, LANES), jnp.float32)] * tiles

    def spread(tile, i):
        return jnp.broadcast_to(tile[i : i + 1, :], (SUBLANES, LANES))

    for start in range(0, count, PANEL):
        stop = min(start + PANEL, count)
        first = start // SUBLANES
        columns = {
            j: {
                g: jnp.broadcast_to(work[g][:, j : j + 1], (SUBLANES, LANES))
                for g in range(first, tiles)
            }
            for j in range(start, stop)
        }
        ahead = spread(columns[start][first], start % SUBLANES)
        for j in range(start, stop):
            i, own = j % SUBLANES, j // SUBLANES
            pivot = ahead
            diagonal[own] = jnp.where(sublane == i, pivot, diagonal[own])
            reciprocal = 1.0 / pivot
            if j + 1 < stop:
                row_next, own_next = (j + 1) % SUBLANES, (j + 1) // SUBLANES
                taken = spread(columns[j][own_next], row_next) * spread(columns[j + 1][own], i)
                ahead = spread(columns[j + 1][own_next], row_next) - taken * reciprocal
            row = spread(work[own], i)
            entries = {k: spread(columns[k][own], i) for k in range(j + 1, stop)}
            for g in range(own, tiles):
                ratio = columns[j][g] * reciprocal
                if g == own:
                    ratio = jnp.where(sublane > i, ratio, 0.0)
                work[g] = work[g] - ratio * row
                for k in range(j + 1, stop):
                    columns[k][g] = columns[k][g] - ratio * entries[k]
    for g in range(tiles):
        scaled = work[g] * lax.rsqrt(diagonal[g])
        inverse_ref[SUBLANES * g : SUBLANES * (g + 1), :] = scaled[:, count : 2 * count]


def basis_kernel(inverse_ref, gram_ref, basis_ref, image_ref, basis_new_ref, image_start_ref, start_ref):
    inverse = inverse_ref[...]
    count, old = inverse.shape[0], image_ref.shape[0]
    basis_new_ref[...] = multiply(inverse, basis_ref[...])
    image_start_ref[...] = multiply(inverse[:, :old], image_ref[...])
    coupling = gram_ref[:, count : count + old]
    start_ref[...] = contract_last(multiply(inverse, coupling), inverse[:, :old])


def image_kernel(scale, basis_new_ref, *refs):
    *sums_refs, image_ref, part_ref = refs
    blocks = sums_refs[0].shape[0]
    summed = pairwise([ref[:blocks] for ref in sums_refs])
    image = jnp.concatenate([summed[b] for b in range(summed.shape[0])], axis=1)
    image_ref[...] = image
    vecs, count = image.shape[0], basis_new_ref.shape[0]
    part = contract_last(image, basis_new_ref[...]) * scale
    part = jnp.concatenate([part, jnp.zeros((vecs, LANES // 2 - count), jnp.float32)], axis=1)
    part = jnp.concatenate([part[: vecs // 2], part[vecs // 2 :]], axis=1)
    part_ref[...] = jnp.broadcast_to(part[None], part_ref.shape)


def finish_kernel(
    inverse_ref, basis_new_ref, image_start_ref, image_ref, start_ref, parts_ref,
    projected_hbm, basis_new_hbm, image_new_hbm, projected_vmem, image_new_vmem, sems,
):
    basis_copy = pltpu.make_async_copy(basis_new_ref, basis_new_hbm, sems.at[0])
    basis_copy.start()
    vecs = image_ref.shape[0]
    count = inverse_ref.shape[0]
    last = inverse_ref[...][:, count - vecs :]
    image_new = image_start_ref[...]
    for k in range(vecs):
        image_new = image_new + last[:, k : k + 1] * image_ref[k : k + 1, :]
    image_new_vmem[...] = image_new
    image_copy = pltpu.make_async_copy(image_new_vmem, image_new_hbm, sems.at[1])
    image_copy.start()
    total = jnp.sum(parts_ref[...], axis=0)
    total = jnp.concatenate([total[:, : LANES // 2], total[:, LANES // 2 :]], axis=0)
    new = lax.dot_general(
        total[:, :count],
        last,
        (((0,), (1,)), ((), ())),
        precision=HIGHEST,
        preferred_element_type=jnp.float32,
    )
    projected_vmem[...] = start_ref[...] + new
    projected_copy = pltpu.make_async_copy(projected_vmem, projected_hbm, sems.at[2])
    projected_copy.start()
    basis_copy.wait()
    image_copy.wait()
    projected_copy.wait()


def call(kernel, outs, *args, after=(), time=0.0, smem=0, from_hbm=False, to_hbm=False, scratch=()):
    operand = pl.BlockSpec(memory_space=pltpu.HBM if from_hbm else pltpu.VMEM)
    result = pl.BlockSpec(memory_space=pltpu.HBM if to_hbm else pltpu.VMEM)
    scalars = pl.BlockSpec(memory_space=pltpu.SMEM)
    if from_hbm:
        args = [pltpu.with_memory_space_constraint(arg, pltpu.HBM) for arg in args]
    result_specs = [scalars if getattr(o, "dtype", None) == jnp.int32 else result for o in outs]
    outs = [o if hasattr(o, "dtype") else jax.ShapeDtypeStruct(o, jnp.float32) for o in outs]
    n_after = len(after)

    def body(*refs):
        kernel(*refs[n_after:])

    return pl.pallas_call(
        body,
        out_shape=outs,
        in_specs=[operand] * n_after + [scalars] * smem + [operand] * (len(args) - smem),
        out_specs=result_specs,
        scratch_shapes=scratch,
        compiler_params=pltpu.CompilerParams(vmem_limit_bytes=VMEM_LIMIT),
        cost_estimate=pl.CostEstimate(
            flops=int(time * FLOPS_PER_US), bytes_accessed=int(time * BYTES_PER_US), transcendentals=0
        ),
        name=(kernel.func if hasattr(kernel, "func") else kernel).__name__[:-7],
    )(*after, *args)


def bits_of(size):
    return [1 << j for j in range(size.bit_length() - 1)]


def swap(array, axis, mask):
    size = lax.axis_size(axis)
    return lax.ppermute(array, axis, [(i, i ^ mask) for i in range(size)])


def local(tile_blocks, tile_rows, tile_cols, trial_vectors, basis_old, image_old):
    tile_size = tile_blocks.shape[1]
    vecs, width = trial_vectors.shape
    old = basis_old.shape[0]
    count = old + vecs
    blocks = width // tile_size
    n_row, n_col = lax.axis_size("row"), lax.axis_size("col")
    scale = 1.0 / float(width * n_row * n_col)
    row_bits, col_bits = [m | 1 for m in bits_of(n_row)], bits_of(n_col)
    gather_row = row_bits[1:] + row_bits[:1]
    scatter_row, scatter_col = row_bits[:1] + row_bits[:0:-1], col_bits
    grams = (count - count // 3) // vecs
    tile = (vecs, tile_size)

    narrow_shape = jax.ShapeDtypeStruct((blocks * vecs, tile_size), trial_vectors.dtype)
    places = pltpu.SMEM(tile_rows.shape, tile_rows.dtype)
    wide, narrow, basis_all, image_kept, rows_kept, cols_kept = call(
        load_kernel,
        [(blocks, *tile), narrow_shape, (count, width), (old, width), places, places],
        trial_vectors,
        basis_old,
        image_old,
        tile_rows,
        tile_cols,
        time=1.0,
        from_hbm=True,
        scratch=[
            pltpu.VMEM((vecs, width), trial_vectors.dtype),
            pltpu.VMEM((old, width), jnp.float32),
            pltpu.SemaphoreType.DMA((5,)),
        ],
    )
    own, again = call(
        functools.partial(gram_kernel, scale),
        [(blocks + grams, *tile), narrow_shape],
        wide,
        narrow,
        basis_all,
        image_kept,
        time=0.5,
    )
    row_got = [swap(own, "col", m) for m in range(1, n_col)]
    col_got = [again]
    for m in gather_row:
        col_got.append(swap(jnp.concatenate(col_got, axis=0), "row", m))

    half_row, half_col = blocks * n_row // 2, blocks * n_col // 2
    col_kept, col_sent = call(
        functools.partial(
            backward_kernel, col_bits, scatter_row[::-1], n_row, blocks, len(row_got)
        ),
        [(half_row, *tile), (half_row + grams, *tile)],
        rows_kept,
        cols_kept,
        tile_blocks,
        own,
        *row_got,
        time=1.0,
        smem=2,
        scratch=[
            pltpu.VMEM((2 * half_col, *tile), jnp.float32),
            pltpu.VMEM((2 * half_row, *tile), jnp.float32),
        ],
    )
    row_kept, row_sent = call(
        functools.partial(
            forward_kernel, scatter_col[::-1], gather_row, n_row, blocks, len(col_got)
        ),
        [(half_col, *tile)] * 2,
        rows_kept,
        cols_kept,
        tile_blocks,
        *col_got,
        time=1.0,
        smem=2,
        scratch=[
            pltpu.VMEM((2 * half_row, *tile), jnp.float32),
            pltpu.VMEM((2 * half_col, *tile), jnp.float32),
        ],
    )
    forward_done = row_kept
    for i, m in enumerate(scatter_row[:-1]):
        half_row //= 2
        col_kept, col_sent = call(
            fold_kernel,
            [(half_row, *tile), (half_row + grams, *tile)],
            col_kept,
            col_sent,
            swap(col_sent, "row", m),
            after=[forward_done] if i == n_row.bit_length() - 3 else [],
            time=0.1,
        )
    col_parts = [col_kept, swap(col_sent, "row", scatter_row[-1])]
    for m in scatter_col[:-1]:
        half_col //= 2
        row_kept, row_sent = call(
            fold_kernel,
            [(half_col, *tile)] * 2,
            row_kept,
            row_sent,
            swap(row_sent, "col", m),
            time=0.1,
        )
    row_parts = [row_kept, swap(row_sent, "col", scatter_col[-1])]

    inverse, gram = call(
        functools.partial(factor_kernel, count, old, blocks),
        [(count, count), (count, LANES)],
        col_sent,
        col_parts[1],
        time=1.1,
    )
    basis_new, image_start, start = call(
        basis_kernel,
        [(count, width), (count, width), (count, count)],
        inverse,
        gram,
        basis_all,
        image_kept,
    )
    image, part = call(
        functools.partial(image_kernel, scale),
        [(vecs, width), (n_row * n_col, vecs // 2, LANES)],
        basis_new,
        *row_parts,
        *col_parts,
    )
    parts = lax.all_to_all(part, ("row", "col"), split_axis=0, concat_axis=0, tiled=True)
    return call(
        finish_kernel,
        [(count, count), (count, width), (count, width)],
        inverse,
        basis_new,
        image_start,
        image,
        start,
        parts,
        to_hbm=True,
        scratch=[
            pltpu.VMEM((count, count), jnp.float32),
            pltpu.VMEM((count, width), jnp.float32),
            pltpu.SemaphoreType.DMA((3,)),
        ],
    )


def solution(mesh):
    in_specs = (
        P(("row", "col"), None, None),
        P(("row", "col")),
        P(("row", "col")),
        P(None, ("col", "row")),
        P(None, ("col", "row")),
        P(None, ("col", "row")),
    )
    out_specs = (P(), P(None, ("col", "row")), P(None, ("col", "row")))
    return jax.shard_map(local, mesh=mesh, in_specs=in_specs, out_specs=out_specs, check_vma=False)
```
